256 devices in a mesh: fsdp: 4 (over y), seq: 64 (over z, x, core).
Axes of the slice: x: 4, y: 4, z: 8, core: 2. Of those that a mesh axis runs over, the one named last changes fastest.
Arguments:
- tokens: bfloat16 [16384, 8192], P('seq', 'fsdp'), may hold values from -400 to 400
- norm_gain: float32 [8192], P('fsdp'), may hold values from 0.1 to 1.9
- in_weight: bfloat16 [8192, 3, 512], P('fsdp'), may hold values from -0.0625 to 0.0625
- short_filter: float32 [512, 3, 3], P('fsdp'), may hold values from -3 to 3
- decay_reach: float32 [512, 16], P('fsdp'), may hold values from 20 to 32768
- mode_freq: float32 [512, 16], P('fsdp'), may hold values from 0.01 to 2.2
- residues: float32 [512, 16], P('fsdp'), may hold values from -1.5 to 1.5
- skip_gain: float32 [512], P('fsdp'), may hold values from -4 to 4
Outputs:
- gated_output: bfloat16 [512, 16384], P('fsdp', 'seq')
The draws below stay inside these ranges and needn't reach their ends.
All inputs are finite; a program needn't handle non-finite values.
Results may differ from the reference program's by a relative error of at most 0.03.
Values may be sent and summed in bfloat16 or wider, within the bound.
No kernel may reach another device: no remote copies, remote signals or barrier semaphores. Data moves between devices by JAX's collectives and lax.ppermute only.
A program may use at most 192 MiB of HBM per device.

```python
import math
import jax
import jax.numpy as jnp
from jax import lax

D = 8192
C = 512
MODES = 16
L = 16384


def column_ramp(rough_key, high_end):
    place = jnp.arange(D, dtype=jnp.float32)[None, :] / (D - 1)
    ramp = jnp.exp(math.log(high_end) * place)
    rough = jax.random.uniform(rough_key, (1, D), jnp.float32, 0.5, 1.0)
    return ramp * rough


def draw_tokens(key, part):
    key = jax.random.fold_in(key, 7)
    base_key, row_key, col_key = jax.random.split(key, 3)
    col_scale = column_ramp(col_key, 10.0)
    row_scale = jnp.exp(jax.random.uniform(row_key, (L, 1), jnp.float32, 0.0, math.log(10.0)))
    base_values = jax.random.truncated_normal(base_key, -4.0, 4.0, (L, D), jnp.float32)
    return (base_values * row_scale * col_scale).astype(jnp.bfloat16)


def levels(key, extent, pieces, smallest, top_value):
    factor_of = 1.0
    for dim, shards_of in pieces:
        steps = jax.random.uniform(jax.random.fold_in(jax.random.fold_in(key, 6), dim), (shards_of,), jnp.float32, smallest / len(pieces), top_value / len(pieces))
        factor_of = factor_of * jnp.repeat(jnp.exp(steps), extent[dim] // shards_of).reshape((-1,) + (1,) * (len(extent) - 1 - dim))
    return factor_of


def centred(key, dims, deviation, most, cuts=(), kind=jnp.bfloat16):
    array = jax.random.normal(key, dims, jnp.float32) * deviation
    if len(cuts) > 0:
        array = levels(key, dims, cuts, -0.22, 0.18) * array
    return jnp.clip(array, min=-most, max=most).astype(kind)


def setup_inputs(seed: int = 0) -> dict:
    arg_keys = jax.random.split(jax.random.key(seed), 9)
    tokens = draw_tokens(jax.random.fold_in(arg_keys[8], 71), 0)
    norm_gain = jnp.clip(1.0 + 0.18 * jax.random.normal(arg_keys[1], (D,), jnp.float32), 0.1, 1.9)
    in_weight = centred(arg_keys[2], (D, 3, C), D ** -0.5, 0.0625, ((0, 4),))
    short_filter = centred(arg_keys[3], (C, 3, 3), 0.6, 3.0, ((0, 4),), jnp.float32)
    decay_reach = jnp.clip(jnp.exp(math.log(32768.0) - 7.4014754 * jax.random.uniform(arg_keys[4], (C, MODES), jnp.float32) ** levels(arg_keys[4], (C, MODES), ((0, 4),), -0.2, 0.2)), 20.0, 32768.0)
    mode_freq = jnp.clip(jnp.exp(math.log(2.2) - 5.3936276 * jax.random.uniform(arg_keys[5], (C, MODES), jnp.float32) ** levels(arg_keys[5], (C, MODES), ((0, 4),), -0.2, 0.2)), 0.01, 2.2)
    residues = centred(arg_keys[6], (C, MODES), MODES ** -0.5, 1.5, ((0, 4),), jnp.float32)
    skip_gain = centred(arg_keys[7], (C,), 1.0, 4.0, ((0, 4),), jnp.float32)
    return {"tokens": tokens, "norm_gain": norm_gain, "in_weight": in_weight, "short_filter": short_filter, "decay_reach": decay_reach, "mode_freq": mode_freq, "residues": residues, "skip_gain": skip_gain}


def reference(tokens, norm_gain, in_weight, short_filter, decay_reach, mode_freq, residues, skip_gain):
    inputs = tokens.astype(jnp.float32)
    inv_rms = lax.rsqrt(lax.optimization_barrier(jnp.mean(inputs * inputs, axis=1, keepdims=True)) + 1e-06)
    normed = (inputs * inv_rms * norm_gain).astype(jnp.bfloat16)
    projected_sum = jnp.dot(normed, in_weight.reshape(D, 3 * C), preferred_element_type=jnp.float32)
    projected = projected_sum.astype(jnp.bfloat16).reshape(L, 3, C).transpose(2, 1, 0)
    padded = jnp.pad(projected.astype(jnp.float32), ((0, 0), (0, 0), (2, 0)))
    streams = short_filter[:, :, 0:1] * padded[:, :, 2:] + short_filter[:, :, 1:2] * padded[:, :, 1:-1] + short_filter[:, :, 2:3] * padded[:, :, :-2]
    gate_stream = streams[:, 0]
    key_stream = streams[:, 1]
    value_stream = streams[:, 2]
    signal = key_stream * value_stream
    positions = jnp.arange(L, dtype=jnp.float32)
    long_filter = jnp.zeros((C, L), jnp.float32)
    for mode_index in range(MODES):
        decay_rate = 1.0 / decay_reach[:, mode_index]
        mode_gain = residues[:, mode_index] * jnp.sqrt(2.0 * decay_rate)
        mode_turn = mode_freq[:, mode_index]
        long_filter = long_filter + mode_gain[:, None] * jnp.exp(-decay_rate[:, None] * positions[None, :]) * jnp.cos(mode_turn[:, None] * positions[None, :])
    spectrum = jnp.fft.rfft(signal, n=2 * L, axis=1) * jnp.fft.rfft(long_filter, n=2 * L, axis=1)
    long_conv = jnp.fft.irfft(spectrum, n=2 * L, axis=1)[:, :L].astype(jnp.float32)
    return (gate_stream * (long_conv + skip_gain[:, None] * signal)).astype(jnp.bfloat16)
```

```python
import functools
import math

import jax
import jax.numpy as jnp
from jax import lax
from jax.experimental import pallas as pl
from jax.experimental.pallas import tpu as pltpu
from jax.sharding import PartitionSpec as P

F32 = jnp.float32
BF16 = jnp.bfloat16
D = 8192
MODES = 16
LANES = 128
TILE = 8
SUB = 64
STEPS = SUB // TILE
LOW = 8
RIM = 16
VMEM = pl.BlockSpec(memory_space=pltpu.VMEM)
SMEM = pl.BlockSpec(memory_space=pltpu.SMEM)


def call(kernel, out_shape, in_specs, scratch=(), limit=40 << 20):
    return pl.pallas_call(
        kernel,
        out_shape=out_shape,
        in_specs=in_specs,
        out_specs=jax.tree.map(lambda _: VMEM, out_shape),
        scratch_shapes=list(scratch),
        compiler_params=pltpu.CompilerParams(vmem_limit_bytes=limit),
    )


def shape(*dims, dtype=F32):
    return jax.ShapeDtypeStruct(dims, dtype)


def cmul(a, b):
    return a[0] * b[0] - a[1] * b[1], a[0] * b[1] + a[1] * b[0]


def turn(angle):
    cycles = jnp.floor(angle * (0.5 / math.pi) + 0.5)
    rest = angle - cycles * 6.28125
    rest = rest - cycles * 1.93500518798828125e-3
    rest = rest - cycles * 3.0199159819e-7
    return jnp.cos(rest), jnp.sin(rest)


def table_kernel(reach_ref, freq_ref, res_ref, p8_ref, r7_ref, gt_ref, p64_ref, low_ref, high_ref, h_ref):
    rate = 1.0 / reach_ref[...]
    freq = freq_ref[...]
    gain = res_ref[...] * jnp.sqrt(2.0 * rate)

    def power(n):
        size = jnp.exp(-rate * n)
        cosine, sine = turn(freq * n)
        return size * cosine, size * sine

    one = (jnp.ones_like(rate), jnp.zeros_like(rate))

    def chain(base, count):
        values = [one]
        for _ in range(count - 1):
            values.append(cmul(values[-1], base))
        return values

    ones = chain(power(1.0), TILE + 1)
    for j in range(TILE):
        for c in range(2):
            r7_ref[:, c, j, :] = ones[TILE - 1 - j][c]
            gt_ref[:, c, j, :] = gain * ones[j + 1][c]
    eights = chain(power(8.0), STEPS)
    for k in range(STEPS):
        for c in range(2):
            p8_ref[k, c] = eights[k][c]
    for q, value in enumerate(chain(power(float(SUB)), 4)):
        for c in range(2):
            p64_ref[q, c] = value[c]
    for ref, n in ((low_ref, 256.0), (high_ref, 2048.0)):
        for k, value in enumerate(chain(power(n), LOW)):
            for c in range(2):
                ref[k, c] = jnp.zeros_like(rate)
                ref[LOW + k, c] = value[c]
    taps = [jnp.zeros((TILE, LANES), F32) for _ in range(STEPS)]
    row = lax.broadcasted_iota(jnp.int32, (TILE, LANES), 0)
    for m in range(MODES):
        real = jnp.where(row == 0, gain[m : m + 1], pltpu.roll(gt_ref[m, 0], 1, 0))
        imag = jnp.where(row == 0, 0.0, pltpu.roll(gt_ref[m, 1], 1, 0))
        for k in range(STEPS):
            taps[k] = taps[k] + (eights[k][0][m : m + 1] * real - eights[k][1][m : m + 1] * imag)
    for k in range(STEPS):
        h_ref[TILE * k : TILE * k + TILE] = taps[k]


def tables(reach, freq, res):
    return call(
        table_kernel,
        (
            shape(STEPS, 2, MODES, LANES),
            shape(MODES, 2, TILE, LANES),
            shape(MODES, 2, TILE, LANES),
            shape(4, 2, MODES, LANES),
            shape(2 * LOW, 2, MODES, LANES),
            shape(2 * LOW, 2, MODES, LANES),
            shape(SUB, LANES),
        ),
        [VMEM] * 3,
    )(reach, freq, res)


def prepare_kernel(tok_ref, rim_ref, gain_ref, xg_ref, ss_ref, acc_ref):
    rows, cols = tok_ref.shape
    gain = gain_ref[...]

    def part(ref, at, to, n):
        x = ref[pl.ds(at, n), :].astype(F32)
        xg_ref[pl.ds(to, n), :] = (x * gain).astype(BF16)
        sq = x * x
        acc_ref[pl.ds(to, n), :] = sum(sq[:, i : i + LANES] for i in range(0, cols, LANES))

    for i in range(0, rows, 32):
        part(tok_ref, i, i, 32)
    part(rim_ref, 0, rows, RIM)
    acc_ref[rows + RIM :] = jnp.zeros((acc_ref.shape[0] - rows - RIM, LANES), F32)
    acc = acc_ref[...]
    high = acc.astype(BF16)
    mid = (acc - high.astype(F32)).astype(BF16)
    ones = jnp.ones((16, LANES), BF16)
    dims = (((1,), (1,)), ((), ()))
    ss_ref[...] = (
        lax.dot_general(ones, high, dims, preferred_element_type=F32)
        + lax.dot_general(ones, mid, dims, preferred_element_type=F32)
    )[:TILE]


def chunk_kernel(step, who_ref, xg_ref, ss_ref, w_ref, out_ref, ext_ref):
    part = (who_ref[0] + step) % 4
    at = pl.ds(pl.multiple_of(part * LANES, LANES), LANES)
    rows = xg_ref.shape[0] - RIM
    ext_ref[...] = jnp.zeros_like(ext_ref)
    for g in range(3):
        got = jnp.dot(xg_ref[...], w_ref[g, :, at], preferred_element_type=F32)
        out_ref[g * rows : (g + 1) * rows] = got[:rows].astype(out_ref.dtype)
        ext_ref[2 * g : 2 * g + 2] = got[rows + RIM - 2 :]
    for i in range(3):
        total = ss_ref[0:1, i * LANES : (i + 1) * LANES]
        high = total.astype(BF16).astype(F32)
        ext_ref[6 + i : 7 + i] = high
        ext_ref[9 + i : 10 + i] = total - high
    out_ref[3 * rows :] = ext_ref[...].astype(out_ref.dtype)


def signal_kernel(a_ref, b_ref, c_ref, d_ref, filt_ref, p8_ref, r7_ref, p64_ref, gate_ref, sig_ref, carry_ref, send_ref, ext_ref, u_ref):
    rows = gate_ref.shape[0]

    def summed(lo, n):
        at = pl.ds(lo, n)
        return a_ref[at, :] + (b_ref[at, :].astype(F32) + c_ref[at, :].astype(F32) + d_ref[at, :].astype(F32))

    tail = summed(3 * rows, RIM)
    inverse = [lax.rsqrt((tail[6 + i : 7 + i] + tail[9 + i : 10 + i]) * (1.0 / D) + 1e-6) for i in range(3)]
    columns = [jnp.broadcast_to(v, (LANES, LANES)).T for v in inverse]
    streams = []
    for g in range(3):
        ext_ref[g, 0:TILE] = jnp.zeros((TILE, LANES), F32)
        rim = tail[2 * g : 2 * g + 2] * columns[2][RIM - 2 : RIM]
        ext_ref[g, TILE - 2 : TILE] = rim.astype(BF16).astype(F32)
        for i in range(rows // LANES):
            value = summed(g * rows + i * LANES, LANES) * columns[i]
            ext_ref[g, pl.ds(TILE + i * LANES, LANES), :] = value.astype(BF16).astype(F32)
        taps = [filt_ref[3 * g + j : 3 * g + j + 1] for j in range(3)]
        streams.append(
            taps[0] * ext_ref[g, pl.ds(TILE, rows), :]
            + taps[1] * ext_ref[g, pl.ds(TILE - 1, rows), :]
            + taps[2] * ext_ref[g, pl.ds(TILE - 2, rows), :]
        )
        if g == 0:
            gate_ref[...] = streams[0]
    sig_ref[...] = streams[1] * streams[2]
    for q in range(rows // SUB):
        tiles = [sig_ref[pl.ds(q * SUB + TILE * k, TILE), :] for k in range(STEPS)]
        for m in range(MODES):
            real = tiles[STEPS - 1]
            imag = jnp.zeros_like(real)
            for k in range(STEPS - 1):
                real = real + p8_ref[STEPS - 1 - k, 0, m : m + 1, :] * tiles[k]
                imag = imag + p8_ref[STEPS - 1 - k, 1, m : m + 1, :] * tiles[k]
            real, imag = cmul((real, imag), (r7_ref[m, 0], r7_ref[m, 1]))
            u_ref[q, 0, m : m + 1, :] = jnp.sum(real, axis=0, keepdims=True)
            u_ref[q, 1, m : m + 1, :] = jnp.sum(imag, axis=0, keepdims=True)
    state = (jnp.zeros((MODES, LANES), F32),) * 2
    step = (p64_ref[1, 0], p64_ref[1, 1])
    for q in range(rows // SUB):
        for c in range(2):
            carry_ref[q, c] = state[c]
        state = cmul(state, step)
        state = (state[0] + u_ref[q, 0], state[1] + u_ref[q, 1])
    for i in range(LOW):
        for c in range(2):
            send_ref[i, c] = state[c].astype(send_ref.dtype)


def weighted(got_ref, table_ref, first, sign):
    real = jnp.zeros((MODES, LANES), F32)
    imag = jnp.zeros((MODES, LANES), F32)
    for i in range(LOW):
        value = (got_ref[i, 0].astype(F32), got_ref[i, 1].astype(F32))
        term = cmul(value, (table_ref[first - i, 0], table_ref[first - i, 1]))
        real, imag = real + term[0], imag + term[1]
    return real, imag


def low_kernel(who_ref, got_ref, low_ref, mine_ref, send_ref):
    mine = weighted(got_ref, low_ref, LOW - 1 + who_ref[1], 1)
    every = weighted(got_ref, low_ref, 2 * LOW - 1, 1)
    for c in range(2):
        mine_ref[c] = mine[c]
        for i in range(LOW):
            send_ref[i, c] = every[c].astype(send_ref.dtype)


def local_kernel(gate_ref, sig_ref, skip_ref, h_ref, out_ref, pad_ref):
    rows = sig_ref.shape[0]
    pad_ref[0:TILE] = jnp.zeros((TILE, LANES), F32)
    for q in range(rows // SUB):
        pad_ref[TILE:] = sig_ref[pl.ds(q * SUB, SUB), :]
        sums = [skip_ref[...] * pad_ref[pl.ds(TILE + TILE * i, TILE), :] for i in range(STEPS)]
        for b in range(TILE):
            moved = [pad_ref[pl.ds(TILE + TILE * i - b, TILE), :] for i in range(STEPS)]
            for a in range(STEPS):
                tap = h_ref[TILE * a + b : TILE * a + b + 1, :]
                for i in range(a, STEPS):
                    sums[i] = sums[i] + tap * moved[i - a]
        for i in range(STEPS):
            at = pl.ds(q * SUB + TILE * i, TILE)
            out_ref[at, :] = gate_ref[at, :] * sums[i]


def final_kernel(who_ref, got_ref, high_ref, low_ref, mine_ref, carry_ref, p64_ref, p8_ref, gt_ref, gate_ref, local_ref, out_ref, e_ref, y_ref):
    rows = gate_ref.shape[0]
    far = weighted(got_ref, high_ref, LOW - 1 + who_ref[2], 1)
    lag = LOW + who_ref[1]
    far = cmul(far, (low_ref[lag, 0], low_ref[lag, 1]))
    enter = (mine_ref[0] + far[0], mine_ref[1] + far[1])
    for q in range(rows // SUB):
        moved = cmul(enter, (p64_ref[q, 0], p64_ref[q, 1])) if q else enter
        for c in range(2):
            e_ref[c] = moved[c] + carry_ref[q, c]
        sums = [jnp.zeros((TILE, LANES), F32) for _ in range(STEPS)]
        for m in range(MODES):
            real, imag = cmul((gt_ref[m, 0], gt_ref[m, 1]), (e_ref[0, m : m + 1, :], e_ref[1, m : m + 1, :]))
            sums[0] = sums[0] + real
            for k in range(1, STEPS):
                sums[k] = sums[k] + (p8_ref[k, 0, m : m + 1, :] * real - p8_ref[k, 1, m : m + 1, :] * imag)
        for k in range(STEPS):
            at = pl.ds(q * SUB + TILE * k, TILE)
            y_ref[at, :] = local_ref[at, :] + gate_ref[at, :] * sums[k]
    out_ref[...] = y_ref[...].T.astype(BF16)


def body(tokens, norm_gain, in_weight, short_filter, decay_reach, mode_freq, residues, skip_gain):
    rows, cols = tokens.shape
    me = lax.axis_index("fsdp").astype(jnp.int32)
    block = lax.axis_index("seq").astype(jnp.int32)
    who = jnp.stack([me, block % LOW, block // LOW])
    count = lax.axis_size("seq")
    fsdp = lax.axis_size("fsdp")

    rim = lax.ppermute(tokens[rows - RIM :], "seq", [(i, i + 1) for i in range(count - 1)])
    xg, ss = call(
        prepare_kernel,
        (shape(rows + RIM, cols, dtype=BF16), shape(TILE, 3 * LANES)),
        [VMEM] * 3,
        [pltpu.VMEM((3 * LANES, LANES), F32)],
    )(tokens, rim, norm_gain[None])
    weight = jnp.transpose(in_weight, (1, 0, 2))

    def chunk(step, dtype):
        return call(
            functools.partial(chunk_kernel, step),
            shape(3 * rows + RIM, LANES, dtype=dtype),
            [SMEM] + [VMEM] * 3,
            [pltpu.VMEM((RIM, LANES), F32)],
        )(who, xg, ss, weight)

    arrived = []
    for step in (2, 1, 3):
        pairs = [(i, (i + step) % fsdp) for i in range(fsdp)]
        arrived.append(lax.ppermute(chunk(step, BF16), "fsdp", pairs))
    own = chunk(0, F32)
    p8, r7, gt, p64, low, high, taps = tables(decay_reach.T, mode_freq.T, residues.T)
    filt = jnp.transpose(short_filter, (1, 2, 0)).reshape(9, LANES)
    gate, signal, carry, send = call(
        signal_kernel,
        (shape(rows, LANES), shape(rows, LANES), shape(4, 2, MODES, LANES), shape(LOW, 2, MODES, LANES, dtype=BF16)),
        [VMEM] * 8,
        [pltpu.VMEM((3, TILE + rows, LANES), F32), pltpu.VMEM((4, 2, MODES, LANES), F32)],
    )(own, *arrived, filt, p8, r7, p64)

    near = [[LOW * g + j for j in range(LOW)] for g in range(count // LOW)]
    got = lax.all_to_all(send, "seq", 0, 0, axis_index_groups=near)
    mine, send = call(
        low_kernel,
        (shape(2, MODES, LANES), shape(LOW, 2, MODES, LANES, dtype=BF16)),
        [SMEM] + [VMEM] * 2,
    )(who, got, low)
    local = call(local_kernel, shape(rows, LANES), [VMEM] * 4, [pltpu.VMEM((TILE + SUB, LANES), F32)])(
        gate, signal, skip_gain[None], taps
    )
    far = [[g + LOW * j for j in range(count // LOW)] for g in range(LOW)]
    got = lax.all_to_all(send, "seq", 0, 0, axis_index_groups=far)
    return call(
        final_kernel,
        shape(LANES, rows, dtype=BF16),
        [SMEM] + [VMEM] * 10,
        [pltpu.VMEM((2, MODES, LANES), F32), pltpu.VMEM((rows, LANES), F32)],
    )(who, got, high, low, mine, carry, p64, p8, gt, gate, local)


def solution(mesh):
    placed = (
        P("seq", "fsdp"),
        P("fsdp"),
        P("fsdp", None, None),
        P("fsdp", None, None),
        P("fsdp", None),
        P("fsdp", None),
        P("fsdp", None),
        P("fsdp"),
    )
    return jax.shard_map(
        body, mesh=mesh, in_specs=placed, out_specs=P("fsdp", "seq"), check_vma=False
    )
```

```python
import math

import jax
import jax.numpy as jnp
from jax import lax
from jax.experimental import pallas as pl
from jax.experimental.pallas import tpu as pltpu
from jax.sharding import PartitionSpec as P

F32 = jnp.float32
BF16 = jnp.bfloat16
D = 8192
MODES = 16
LANES = 128
TILE = 8
SUB = 64
STEPS = SUB // TILE
LOW = 8
PLANES = 8
HEAD = 2 * MODES
TAIL = HEAD + 4
EXTRA = 16
WIRE = 48
VMEM = pl.BlockSpec(memory_space=pltpu.VMEM)
HBM = pl.BlockSpec(memory_space=pltpu.HBM)


def call(kernel, out_shape, operands, scratch=(), limit=16 << 20, flops=0, places=None):
    moved = sum(math.prod(v.shape) * v.dtype.itemsize for v in (*operands, *jax.tree.leaves(out_shape)))
    return pl.pallas_call(
        kernel,
        out_shape=out_shape,
        in_specs=places or [VMEM] * len(operands),
        out_specs=jax.tree.map(lambda _: VMEM, out_shape),
        scratch_shapes=list(scratch),
        compiler_params=pltpu.CompilerParams(vmem_limit_bytes=limit),
        cost_estimate=pl.CostEstimate(flops=flops, bytes_accessed=moved, transcendentals=0),
    )(*operands)


def shape(*dims, dtype=F32):
    return jax.ShapeDtypeStruct(dims, dtype)


def cmul(a, b):
    return a[0] * b[0] - a[1] * b[1], a[0] * b[1] + a[1] * b[0]


def turn(angle):
    cycles = jnp.floor(angle * (0.5 / math.pi) + 0.5)
    rest = angle - cycles * 6.28125
    rest = rest - cycles * 1.93500518798828125e-3
    rest = rest - cycles * 3.0199159819e-7
    return jnp.cos(rest), jnp.sin(rest)


def table_kernel(
    reach_ref, freq_ref, res_ref, p8_ref, r7_ref, gt_ref, p64_ref, mine_ref, all_ref, far_ref, plane_ref, h_ref, before_ref, power_ref
):
    rate = 1.0 / reach_ref[...]
    freq = freq_ref[...]
    gain = res_ref[...] * jnp.sqrt(2.0 * rate)
    block = lax.axis_index("seq")
    place = lax.rem(block, LOW)
    plane = lax.div(block, LOW)

    def power(n):
        size = jnp.exp(-rate * n)
        cosine, sine = turn(freq * n)
        return size * cosine, size * sine

    one = (jnp.ones_like(rate), jnp.zeros_like(rate))

    def chain(base, count):
        values = [one]
        for _ in range(count - 1):
            values.append(cmul(values[-1], base))
        return values

    ones = chain(power(1.0), TILE + 1)
    for j in range(TILE):
        for c in range(2):
            r7_ref[:, c, j, :] = ones[TILE - 1 - j][c]
            gt_ref[:, c, j, :] = gain * ones[j + 1][c]
    eights = chain(power(8.0), STEPS)
    for k in range(STEPS):
        for c in range(2):
            p8_ref[k, c] = eights[k][c]
    for q, value in enumerate(chain(power(float(SUB)), 4)):
        for c in range(2):
            p64_ref[q, c] = value[c]
    blocks = chain(power(256.0), LOW)
    for k, value in enumerate(blocks):
        for c in range(2):
            power_ref[k, c] = jnp.zeros_like(rate)
            power_ref[LOW + k, c] = value[c]
    for i in range(LOW):
        for c in range(2):
            mine_ref[i, c] = power_ref[LOW - 1 - i + place, c]
            all_ref[i, c] = blocks[LOW - 1 - i][c]
    unit, far = power(1.0), power(2048.0)
    size = jnp.exp(2.0 * rate)
    back = (size * unit[0], -size * unit[1])
    twice = cmul(back, back)
    last = cmul(blocks[1], back)
    earlier = cmul(last, back)
    rows = (
        (power_ref[LOW + place, 0], power_ref[LOW + place, 1]),
        (power_ref[LOW - 1 + place, 0], power_ref[LOW - 1 + place, 1]),
        far,
        last,
        earlier,
        cmul(last, blocks[LOW - 1]),
        cmul(earlier, blocks[LOW - 1]),
        back,
        twice,
    )
    for i, value in enumerate(rows):
        for c in range(2):
            plane_ref[i, c] = value[c]
    for k, value in enumerate(chain(far, PLANES)):
        for c in range(2):
            power_ref[LOW + k, c] = value[c]
    for i in range(PLANES):
        for c in range(2):
            far_ref[i, c] = power_ref[LOW - 1 - i + plane, c]
    before_ref[...] = jnp.sum(gain * back[0], axis=0, keepdims=True)
    taps = [jnp.zeros((TILE, LANES), F32) for _ in range(STEPS)]
    row = lax.broadcasted_iota(jnp.int32, (TILE, LANES), 0)
    for m in range(MODES):
        real = jnp.where(row == 0, gain[m : m + 1], pltpu.roll(gt_ref[m, 0], 1, 0))
        imag = jnp.where(row == 0, 0.0, pltpu.roll(gt_ref[m, 1], 1, 0))
        for k in range(STEPS):
            taps[k] = taps[k] + (eights[k][0][m : m + 1] * real - eights[k][1][m : m + 1] * imag)
    for k in range(STEPS):
        h_ref[TILE * k : TILE * k + TILE] = taps[k]


def project_kernel(
    tok_hbm, gain_hbm, w_hbm, two_ref, one_ref, three_ref, own_ref,
    tok_ref, gain_ref, w_ref, xg_ref, acc_ref, ext_ref, got_ref, sems, w_sems,
):
    rows, cols = tok_ref.shape
    outs = {2: two_ref, 1: one_ref, 3: three_ref, 0: own_ref}
    pieces = 4
    span = rows // pieces
    gain_copy = pltpu.make_async_copy(gain_hbm, gain_ref, sems.at[0])
    gain_copy.start()
    tok_copies = []
    for i in range(pieces):
        at = pl.ds(i * span, span)
        tok_copies.append(pltpu.make_async_copy(tok_hbm.at[at], tok_ref.at[at], sems.at[1 + i]))
        tok_copies[-1].start(priority=i % 2)
    w_copies = [pltpu.make_async_copy(w_hbm.at[g], w_ref.at[g], w_sems.at[g]) for g in range(3)]
    w_copies[0].start(priority=0)
    w_copies[1].start(priority=1)
    gain_copy.wait()
    gain = gain_ref[...]
    for i in range(pieces):
        tok_copies[i].wait()
        if i == 1:
            w_copies[2].start(priority=0)
        for lo in range(i * span, (i + 1) * span, 32):
            x = tok_ref[pl.ds(lo, 32), :].astype(F32)
            xg_ref[pl.ds(lo, 32), :] = (x * gain).astype(BF16)
            sq = x * x
            acc_ref[pl.ds(lo, 32), :] = sum(sq[:, j : j + LANES] for j in range(0, cols, LANES))
    acc = acc_ref[...]
    high = acc.astype(BF16)
    mid = (acc - high.astype(F32)).astype(BF16)
    ones = jnp.ones((16, LANES), BF16)
    dims = (((1,), (1,)), ((), ()))
    total = (
        lax.dot_general(ones, high, dims, preferred_element_type=F32)
        + lax.dot_general(ones, mid, dims, preferred_element_type=F32)
    )[:1]
    ext_ref[...] = jnp.zeros_like(ext_ref)
    for i in range(rows // LANES):
        value = total[:, i * LANES : (i + 1) * LANES]
        high = value.astype(BF16).astype(F32)
        ext_ref[i : i + 1] = high
        ext_ref[2 + i : 3 + i] = value - high
    for out in outs.values():
        out[3 * rows :] = ext_ref[...].astype(out.dtype)
    me = lax.axis_index("fsdp")
    for g in range(3):
        w_copies[g].wait()
        got_ref[...] = jnp.dot(xg_ref[...], w_ref[g], preferred_element_type=F32)
        for d, out in outs.items():
            at = pl.ds(pl.multiple_of(lax.rem(me + d, 4) * LANES, LANES), LANES)
            out[g * rows : (g + 1) * rows] = got_ref[:, at].astype(out.dtype)


def local(sig_ref, skip_ref, h_ref, out_ref, pad_ref):
    pad_ref[0:TILE] = jnp.zeros((TILE, LANES), F32)
    for q in range(sig_ref.shape[0] // SUB):
        pad_ref[TILE:] = sig_ref[pl.ds(q * SUB, SUB), :]
        sums = [skip_ref[...] * pad_ref[pl.ds(TILE + TILE * i, TILE), :] for i in range(STEPS)]
        for b in range(TILE):
            moved = [pad_ref[pl.ds(TILE + TILE * i - b, TILE), :] for i in range(STEPS)]
            for a in range(STEPS):
                tap = h_ref[TILE * a + b : TILE * a + b + 1, :]
                for i in range(a, STEPS):
                    sums[i] = sums[i] + tap * moved[i - a]
        for i in range(STEPS):
            out_ref[pl.ds(q * SUB + TILE * i, TILE), :] = sums[i]


def signal_kernel(
    a_ref, b_ref, c_ref, d_ref, filt_ref, p8_ref, r7_ref, p64_ref, skip_ref, h_ref,
    gate_ref, local_ref, carry_ref, send_ref, head_ref, ext_ref, u_ref, wire_ref, sig_ref, pad_ref,
):
    rows = gate_ref.shape[0]
    subs = rows // SUB

    def summed(lo, n):
        at = pl.ds(lo, n)
        return a_ref[at, :] + (b_ref[at, :].astype(F32) + c_ref[at, :].astype(F32) + d_ref[at, :].astype(F32))

    tail = summed(3 * rows, EXTRA)
    inverse = [lax.rsqrt((tail[i : i + 1] + tail[2 + i : 3 + i]) * (1.0 / D) + 1e-6) for i in range(rows // LANES)]
    columns = [jnp.broadcast_to(v, (LANES, LANES)).T for v in inverse]
    streams = []
    for g in range(3):
        ext_ref[g, 0:TILE] = jnp.zeros((TILE, LANES), F32)
        for i in range(rows // LANES):
            value = summed(g * rows + i * LANES, LANES) * columns[i]
            ext_ref[g, pl.ds(TILE + i * LANES, LANES), :] = value.astype(BF16).astype(F32)
        taps = [filt_ref[3 * g + j : 3 * g + j + 1] for j in range(3)]
        streams.append(
            taps[0] * ext_ref[g, pl.ds(TILE, rows), :]
            + taps[1] * ext_ref[g, pl.ds(TILE - 1, rows), :]
            + taps[2] * ext_ref[g, pl.ds(TILE - 2, rows), :]
        )
        if g == 0:
            gate_ref[...] = streams[0]
    for g in range(3):
        head_ref[2 * g : 2 * g + 2] = streams[g][:2]
    head_ref[6:] = jnp.zeros((2, LANES), F32)
    signal = streams[1] * streams[2]
    row = lax.broadcasted_iota(jnp.int32, (rows, LANES), 0)
    sig_ref[...] = jnp.where(row < 2, 0.0, signal)
    wire_ref[HEAD:] = jnp.zeros((WIRE - HEAD, LANES), F32)
    for i, (g, at) in enumerate(((1, 0), (2, 0), (1, rows - 2), (2, rows - 2), (0, rows - 2))):
        wire_ref[HEAD + 2 * i : HEAD + 2 * i + 2] = ext_ref[g, TILE + at : TILE + at + 2]
    tiles = [[sig_ref[pl.ds(q * SUB + TILE * k, TILE), :] for k in range(STEPS)] for q in range(subs)]
    for m in range(MODES):
        real = [tiles[q][STEPS - 1] for q in range(subs)]
        imag = [None] * subs
        for k in range(STEPS - 1):
            by = [p8_ref[STEPS - 1 - k, c, m : m + 1, :] for c in range(2)]
            for q in range(subs):
                real[q] = real[q] + by[0] * tiles[q][k]
                term = by[1] * tiles[q][k]
                imag[q] = term if k == 0 else imag[q] + term
        for q in range(subs):
            turned = cmul((real[q], imag[q]), (r7_ref[m, 0], r7_ref[m, 1]))
            for c in range(2):
                u_ref[q, c, m : m + 1, :] = jnp.sum(turned[c], axis=0, keepdims=True)
    state = (jnp.zeros((MODES, LANES), F32),) * 2
    step = (p64_ref[1, 0], p64_ref[1, 1])
    for q in range(subs):
        for c in range(2):
            carry_ref[q, c] = state[c]
        state = cmul(state, step)
        state = (state[0] + u_ref[q, 0], state[1] + u_ref[q, 1])
    for c in range(2):
        wire_ref[MODES * c : MODES * (c + 1)] = state[c]
    wire = wire_ref[...].astype(send_ref.dtype)
    for i in range(LOW):
        send_ref[i] = wire
    local(sig_ref, skip_ref, h_ref, local_ref, pad_ref)


def edges(filt_ref, first, rim):
    def stream(g, own, old):
        taps = [filt_ref[3 * g + j : 3 * g + j + 1] for j in range(3)]
        return (
            taps[0] * own[0] + taps[1] * old[1] + taps[2] * old[0],
            taps[0] * own[1] + taps[1] * own[0] + taps[2] * old[1],
        )

    keys = stream(1, first[:2], rim[:2])
    values = stream(2, first[2:], rim[2:4])
    return keys[0] * values[0], keys[1] * values[1]


def lines(ref, at, count):
    return [ref[at + i : at + i + 1] for i in range(count)]


def impulses(plane_ref, at, pair):
    return [plane_ref[at, c] * pair[0] + plane_ref[at + 1, c] * pair[1] for c in range(2)]


def gathered(got_ref, wide_ref, plane_ref, at, filt_ref, tables, alone):
    zero = jnp.zeros((MODES, LANES), F32)
    sums = [[zero, zero] for _ in tables]
    for i in range(got_ref.shape[0]):
        wide_ref[i] = got_ref[i].astype(F32)
        value = [wide_ref[i, 0:MODES], wide_ref[i, MODES:HEAD]]
        if i or alone:
            rim = lines(wide_ref.at[i - 1], TAIL, 4) if i else [0.0] * 4
            extra = impulses(plane_ref, at, edges(filt_ref, lines(wide_ref.at[i], HEAD, 4), rim))
            value = [value[0] + extra[0], value[1] + extra[1]]
        for total, table_ref in zip(sums, tables):
            term = cmul(value, (table_ref[i, 0], table_ref[i, 1]))
            total[0], total[1] = total[0] + term[0], total[1] + term[1]
    return sums


def plane_kernel(got_ref, mine_tab_ref, all_tab_ref, plane_ref, filt_ref, mine_ref, rim_ref, send_ref, wide_ref, wire_ref):
    mine, total = gathered(got_ref, wide_ref, plane_ref, 3, filt_ref, (mine_tab_ref, all_tab_ref), False)
    place = lax.rem(lax.axis_index("seq"), LOW)
    near = wide_ref[jnp.maximum(place - 1, 0), TAIL : TAIL + TILE]
    rim_ref[0] = jnp.where(place > 0, near, 0.0)
    rim_ref[1] = wide_ref[0, HEAD : HEAD + TILE]
    for c in range(2):
        mine_ref[c] = mine[c]
        wire_ref[c * MODES : (c + 1) * MODES] = total[c]
    wire_ref[HEAD:TAIL] = wide_ref[0, HEAD:TAIL]
    wire_ref[TAIL:] = wide_ref[LOW - 1, TAIL:]
    wire = wire_ref[...].astype(send_ref.dtype)
    for i in range(PLANES):
        send_ref[i] = wire


def final_kernel(
    got_ref, far_tab_ref, rim_ref, plane_ref, filt_ref, mine_ref, carry_ref, p64_ref, p8_ref, gt_ref, gate_ref, local_ref,
    head_ref, skip_ref, before_ref, out_ref, wide_ref, e_ref, y_ref, fix_ref,
):
    rows = gate_ref.shape[0]
    subs = rows // SUB
    (far,) = gathered(got_ref, wide_ref, plane_ref, 5, filt_ref, (far_tab_ref,), True)
    far = cmul(far, (plane_ref[0, 0], plane_ref[0, 1]))
    block = lax.axis_index("seq")
    place, plane = lax.rem(block, LOW), lax.div(block, LOW)
    old = jnp.where(plane > 0, wide_ref[jnp.maximum(plane - 1, 0), TAIL : TAIL + TILE], 0.0)
    extra = impulses(plane_ref, 3, edges(filt_ref, lines(rim_ref.at[1], 0, 4), [old[i : i + 1] for i in range(4)]))
    near = cmul(extra, (plane_ref[1, 0], plane_ref[1, 1]))
    rim = rim_ref[0] + jnp.where(place > 0, 0.0, old)
    old = {1: (rim[0:1], rim[1:2]), 2: (rim[2:3], rim[3:4]), 0: (rim[4:5], rim[5:6])}
    late = {}
    for g in range(3):
        taps = [filt_ref[3 * g + j : 3 * g + j + 1] for j in range(3)]
        late[g] = (taps[1] * old[g][1] + taps[2] * old[g][0], taps[2] * old[g][1])
    pair = [
        (head_ref[2 + i : 3 + i] + late[1][i]) * (head_ref[4 + i : 5 + i] + late[2][i]) for i in range(2)
    ]
    own = impulses(plane_ref, 7, pair)
    enter = [mine_ref[c] + near[c] + far[c] + own[c] for c in range(2)]
    fix_ref[...] = jnp.zeros_like(fix_ref)
    for i in range(2):
        fix_ref[0, i : i + 1] = late[0][i]
        fix_ref[1, i : i + 1] = skip_ref[...] * pair[i]
    fix_ref[1, 0:1] -= before_ref[...] * pair[1]
    for q in range(subs):
        moved = cmul(enter, (p64_ref[q, 0], p64_ref[q, 1])) if q else enter
        for c in range(2):
            e_ref[q, c] = moved[c] + carry_ref[q, c]
    sums = [[None] * STEPS for _ in range(subs)]
    for m in range(MODES):
        table = (gt_ref[m, 0], gt_ref[m, 1])
        value = [cmul(table, (e_ref[q, 0, m : m + 1, :], e_ref[q, 1, m : m + 1, :])) for q in range(subs)]
        for k in range(STEPS):
            if k:
                by = [p8_ref[k, c, m : m + 1, :] for c in range(2)]
            for q in range(subs):
                term = by[0] * value[q][0] - by[1] * value[q][1] if k else value[q][0]
                sums[q][k] = term if m == 0 else sums[q][k] + term
    for q in range(subs):
        for k in range(STEPS):
            at = pl.ds(q * SUB + TILE * k, TILE)
            gate, conv = gate_ref[at, :], local_ref[at, :] + sums[q][k]
            if q == 0 and k == 0:
                gate, conv = gate + fix_ref[0], conv + fix_ref[1]
            y_ref[at, :] = gate * conv
    out_ref[...] = y_ref[...].T.astype(BF16)


def body(tokens, norm_gain, in_weight, short_filter, decay_reach, mode_freq, residues, skip_gain):
    rows, cols = tokens.shape
    fsdp = lax.axis_size("fsdp")
    state = shape(2, MODES, LANES)

    packed = 3 * rows + EXTRA
    weight = jnp.transpose(in_weight, (1, 0, 2))
    block = shape(packed, LANES, dtype=BF16)
    *sent, own = call(
        project_kernel,
        (block, block, block, shape(packed, LANES)),
        (tokens, pltpu.with_memory_space_constraint(norm_gain[None], pltpu.HBM), weight),
        [
            pltpu.VMEM((rows, cols), BF16),
            pltpu.VMEM((1, cols), F32),
            pltpu.VMEM((3, cols, 4 * LANES), BF16),
            pltpu.VMEM((rows, cols), BF16),
            pltpu.VMEM((rows, LANES), F32),
            pltpu.VMEM((EXTRA, LANES), F32),
            pltpu.VMEM((rows, 4 * LANES), F32),
            pltpu.SemaphoreType.DMA((5,)),
            pltpu.SemaphoreType.DMA((3,)),
        ],
        limit=52 << 20,
        flops=2 * rows * cols * 12 * LANES,
        places=[HBM] * 3,
    )
    arrived = [
        lax.ppermute(part, "fsdp", [(i, (i + step) % fsdp) for i in range(fsdp)])
        for step, part in zip((2, 1, 3), sent)
    ]
    p8, r7, gt, p64, mine_tab, all_tab, far_tab, plane_tab, taps, before = call(
        table_kernel,
        (
            shape(STEPS, 2, MODES, LANES),
            shape(MODES, 2, TILE, LANES),
            shape(MODES, 2, TILE, LANES),
            shape(4, 2, MODES, LANES),
            shape(LOW, 2, MODES, LANES),
            shape(LOW, 2, MODES, LANES),
            shape(PLANES, 2, MODES, LANES),
            shape(9, 2, MODES, LANES),
            shape(SUB, LANES),
            shape(1, LANES),
        ),
        (decay_reach.T, mode_freq.T, residues.T),
        [pltpu.VMEM((2 * LOW, 2, MODES, LANES), F32)],
        flops=1 << 27,
    )
    filt = jnp.transpose(short_filter, (1, 2, 0)).reshape(9, LANES)
    skip = skip_gain[None]
    wire = shape(LOW, WIRE, LANES, dtype=BF16)
    gate, local_part, carry, send, head = call(
        signal_kernel,
        (shape(rows, LANES), shape(rows, LANES), shape(4, 2, MODES, LANES), wire, shape(TILE, LANES)),
        (own, *arrived, filt, p8, r7, p64, skip, taps),
        [
            pltpu.VMEM((3, TILE + rows, LANES), F32),
            pltpu.VMEM((4, 2, MODES, LANES), F32),
            pltpu.VMEM((WIRE, LANES), F32),
            pltpu.VMEM((rows, LANES), F32),
            pltpu.VMEM((TILE + SUB, LANES), F32),
        ],
        flops=1 << 27,
    )
    plane = [[LOW * g + j for j in range(LOW)] for g in range(PLANES)]
    got = lax.all_to_all(send, "seq", 0, 0, axis_index_groups=plane)
    mine, rim, send = call(
        plane_kernel,
        (state, shape(2, TILE, LANES), wire),
        (got, mine_tab, all_tab, plane_tab, filt),
        [pltpu.VMEM((LOW, WIRE, LANES), F32), pltpu.VMEM((WIRE, LANES), F32)],
        flops=1 << 24,
    )
    line = [[LOW * j + g for j in range(PLANES)] for g in range(LOW)]
    got = lax.all_to_all(send, "seq", 0, 0, axis_index_groups=line)
    return call(
        final_kernel,
        shape(LANES, rows, dtype=BF16),
        (got, far_tab, rim, plane_tab, filt, mine, carry, p64, p8, gt, gate, local_part, head, skip, before),
        [
            pltpu.VMEM((PLANES, WIRE, LANES), F32),
            pltpu.VMEM((4, 2, MODES, LANES), F32),
            pltpu.VMEM((rows, LANES), F32),
            pltpu.VMEM((2, TILE, LANES), F32),
        ],
        flops=1 << 27,
    )


def solution(mesh):
    placed = (
        P("seq", "fsdp"),
        P("fsdp"),
        P("fsdp", None, None),
        P("fsdp", None, None),
        P("fsdp", None),
        P("fsdp", None),
        P("fsdp", None),
        P("fsdp"),
    )
    return jax.shard_map(
        body, mesh=mesh, in_specs=placed, out_specs=P("fsdp", "seq"), check_vma=False
    )
```

```python
import math

import jax
import jax.numpy as jnp
from jax import lax
from jax.experimental import pallas as pl
from jax.experimental.pallas import tpu as pltpu
from jax.sharding import PartitionSpec as P

F32 = jnp.float32
BF16 = jnp.bfloat16
D = 8192
MODES = 16
LANES = 128
TILE = 8
SUB = 64
STEPS = SUB // TILE
LOW = 8
PLANES = 8
HEAD = 2 * MODES
TAIL = HEAD + 4
EXTRA = 16
WIRE = 48
VMEM = pl.BlockSpec(memory_space=pltpu.VMEM)
HBM = pl.BlockSpec(memory_space=pltpu.HBM)


def call(kernel, out_shape, operands, scratch=(), limit=16 << 20, flops=0, places=None):
    moved = sum(math.prod(v.shape) * v.dtype.itemsize for v in (*operands, *jax.tree.leaves(out_shape)))
    return pl.pallas_call(
        kernel,
        out_shape=out_shape,
        in_specs=places or [VMEM] * len(operands),
        out_specs=jax.tree.map(lambda _: VMEM, out_shape),
        scratch_shapes=list(scratch),
        compiler_params=pltpu.CompilerParams(vmem_limit_bytes=limit),
        cost_estimate=pl.CostEstimate(flops=flops, bytes_accessed=moved, transcendentals=0),
    )(*operands)


def shape(*dims, dtype=F32):
    return jax.ShapeDtypeStruct(dims, dtype)


def cmul(a, b):
    return a[0] * b[0] - a[1] * b[1], a[0] * b[1] + a[1] * b[0]


def turn(angle):
    cycles = jnp.floor(angle * (0.5 / math.pi) + 0.5)
    rest = angle - cycles * 6.28125
    rest = rest - cycles * 1.93500518798828125e-3
    rest = rest - cycles * 3.0199159819e-7
    return jnp.cos(rest), jnp.sin(rest)


def table_kernel(
    reach_ref, freq_ref, res_ref, p8_ref, r7_ref, gt_ref, p64_ref, mine_ref, all_ref, far_ref, plane_ref, h_ref, before_ref, power_ref
):
    rate = 1.0 / reach_ref[...]
    freq = freq_ref[...]
    gain = res_ref[...] * jnp.sqrt(2.0 * rate)
    block = lax.axis_index("seq")
    place = lax.rem(block, LOW)
    plane = lax.div(block, LOW)

    def power(n):
        size = jnp.exp(-rate * n)
        cosine, sine = turn(freq * n)
        return size * cosine, size * sine

    one = (jnp.ones_like(rate), jnp.zeros_like(rate))

    def chain(base, count):
        values = [one]
        for _ in range(count - 1):
            values.append(cmul(values[-1], base))
        return values

    ones = chain(power(1.0), TILE + 1)
    for j in range(TILE):
        for c in range(2):
            r7_ref[:, c, j, :] = ones[TILE - 1 - j][c]
            gt_ref[:, c, j, :] = gain * ones[j + 1][c]
    eights = chain(power(8.0), STEPS)
    for k in range(STEPS):
        for c in range(2):
            p8_ref[k, c] = eights[k][c]
    for q, value in enumerate(chain(power(float(SUB)), 4)):
        for c in range(2):
            p64_ref[q, c] = value[c]
    blocks = chain(power(256.0), LOW)
    for k, value in enumerate(blocks):
        for c in range(2):
            power_ref[k, c] = jnp.zeros_like(rate)
            power_ref[LOW + k, c] = value[c]
    for i in range(LOW):
        for c in range(2):
            mine_ref[i, c] = power_ref[LOW - 1 - i + place, c]
            all_ref[i, c] = blocks[LOW - 1 - i][c]
    unit, far = power(1.0), power(2048.0)
    size = jnp.exp(2.0 * rate)
    back = (size * unit[0], -size * unit[1])
    twice = cmul(back, back)
    last = cmul(blocks[1], back)
    earlier = cmul(last, back)
    rows = (
        (power_ref[LOW + place, 0], power_ref[LOW + place, 1]),
        (power_ref[LOW - 1 + place, 0], power_ref[LOW - 1 + place, 1]),
        far,
        last,
        earlier,
        cmul(last, blocks[LOW - 1]),
        cmul(earlier, blocks[LOW - 1]),
        back,
        twice,
    )
    for i, value in enumerate(rows):
        for c in range(2):
            plane_ref[i, c] = value[c]
    for k, value in enumerate(chain(far, PLANES)):
        for c in range(2):
            power_ref[LOW + k, c] = value[c]
    for i in range(PLANES):
        for c in range(2):
            far_ref[i, c] = power_ref[LOW - 1 - i + plane, c]
    before_ref[...] = jnp.sum(gain * back[0], axis=0, keepdims=True)
    taps = [jnp.zeros((TILE, LANES), F32) for _ in range(STEPS)]
    row = lax.broadcasted_iota(jnp.int32, (TILE, LANES), 0)
    for m in range(MODES):
        real = jnp.where(row == 0, gain[m : m + 1], pltpu.roll(gt_ref[m, 0], 1, 0))
        imag = jnp.where(row == 0, 0.0, pltpu.roll(gt_ref[m, 1], 1, 0))
        for k in range(STEPS):
            taps[k] = taps[k] + (eights[k][0][m : m + 1] * real - eights[k][1][m : m + 1] * imag)
    for k in range(STEPS):
        h_ref[TILE * k : TILE * k + TILE] = taps[k]


def project_kernel(
    tok_hbm, gain_hbm, w_hbm, own_ref, one_ref, two_ref, three_ref, own_gate, one_gate, two_gate, three_gate,
    tok_ref, gain_ref, w_ref, xg_ref, acc_ref, ext_ref, got_ref, sems, w_sems,
):
    rows, cols = tok_ref.shape
    outs = (own_ref, one_ref, two_ref, three_ref)
    gates = (own_gate, one_gate, two_gate, three_gate)
    pieces = 4
    span = rows // pieces
    gain_copy = pltpu.make_async_copy(gain_hbm, gain_ref, sems.at[0])
    gain_copy.start()
    tok_copies = []
    for i in range(pieces):
        at = pl.ds(i * span, span)
        tok_copies.append(pltpu.make_async_copy(tok_hbm.at[at], tok_ref.at[at], sems.at[1 + i]))
        tok_copies[-1].start(priority=i % 2)
    w_copies = [pltpu.make_async_copy(w_hbm.at[(g + 1) % 3], w_ref.at[g], w_sems.at[g]) for g in range(3)]
    w_copies[0].start(priority=0)
    w_copies[1].start(priority=1)
    gain_copy.wait()
    gain = gain_ref[...]
    for i in range(pieces):
        tok_copies[i].wait()
        if i == 1:
            w_copies[2].start(priority=0)
        for lo in range(i * span, (i + 1) * span, 32):
            x = tok_ref[pl.ds(lo, 32), :].astype(F32)
            xg_ref[pl.ds(lo, 32), :] = (x * gain).astype(BF16)
            sq = x * x
            acc_ref[pl.ds(lo, 32), :] = sum(sq[:, j : j + LANES] for j in range(0, cols, LANES))
    acc = acc_ref[...]
    high = acc.astype(BF16)
    mid = (acc - high.astype(F32)).astype(BF16)
    ones = jnp.ones((16, LANES), BF16)
    dims = (((1,), (1,)), ((), ()))
    total = (
        lax.dot_general(ones, high, dims, preferred_element_type=F32)
        + lax.dot_general(ones, mid, dims, preferred_element_type=F32)
    )[:1]
    ext_ref[...] = jnp.zeros_like(ext_ref)
    for i in range(rows // LANES):
        value = total[:, i * LANES : (i + 1) * LANES]
        high = value.astype(BF16).astype(F32)
        ext_ref[i : i + 1] = high
        ext_ref[2 + i : 3 + i] = value - high
    me = lax.axis_index("fsdp")
    for g in range(3):
        w_copies[g].wait()
        got_ref[...] = jnp.dot(xg_ref[...], w_ref[g], preferred_element_type=F32)
        for d in range(4):
            at = pl.ds(pl.multiple_of(lax.rem(me + d, 4) * LANES, LANES), LANES)
            if g < 2:
                outs[d][g * rows : (g + 1) * rows] = got_ref[:, at].astype(outs[d].dtype)
            else:
                gates[d][...] = got_ref[:, at].astype(gates[d].dtype)
                ext_ref[4:6] = got_ref[rows - 2 : rows, at]
                outs[d][2 * rows :] = ext_ref[...].astype(outs[d].dtype)


def local_kernel(sig_ref, skip_ref, h_ref, _, out_ref, pad_ref):
    pad_ref[0:TILE] = jnp.zeros((TILE, LANES), F32)
    for q in range(sig_ref.shape[0] // SUB):
        pad_ref[TILE:] = sig_ref[pl.ds(q * SUB, SUB), :]
        sums = [skip_ref[...] * pad_ref[pl.ds(TILE + TILE * i, TILE), :] for i in range(STEPS)]
        for b in range(TILE):
            moved = [pad_ref[pl.ds(TILE + TILE * i - b, TILE), :] for i in range(STEPS)]
            for a in range(STEPS):
                tap = h_ref[TILE * a + b : TILE * a + b + 1, :]
                for i in range(a, STEPS):
                    sums[i] = sums[i] + tap * moved[i - a]
        for i in range(STEPS):
            out_ref[pl.ds(q * SUB + TILE * i, TILE), :] = sums[i]


def summed(refs, lo, n):
    at = pl.ds(lo, n)
    return refs[0][at, :] + (refs[1][at, :].astype(F32) + refs[2][at, :].astype(F32) + refs[3][at, :].astype(F32))


def stream(refs, lo, scale_ref, filt_ref, g, ext_ref):
    rows = scale_ref.shape[0]
    ext_ref[0:TILE] = jnp.zeros((TILE, LANES), F32)
    for i in range(0, rows, LANES):
        value = summed(refs, lo + i, LANES) * scale_ref[pl.ds(i, LANES), :]
        ext_ref[pl.ds(TILE + i, LANES), :] = value.astype(BF16).astype(F32)
    taps = [filt_ref[3 * g + j : 3 * g + j + 1] for j in range(3)]
    return (
        taps[0] * ext_ref[pl.ds(TILE, rows), :]
        + taps[1] * ext_ref[pl.ds(TILE - 1, rows), :]
        + taps[2] * ext_ref[pl.ds(TILE - 2, rows), :]
    )


def signal_kernel(
    a_ref, b_ref, c_ref, d_ref, filt_ref, p8_ref, r7_ref, p64_ref,
    scale_ref, sig_ref, carry_ref, send_ref, head_ref, ext_ref, u_ref, wire_ref,
):
    rows = sig_ref.shape[0]
    subs = rows // SUB
    refs = (a_ref, b_ref, c_ref, d_ref)
    tail = summed(refs, 2 * rows, EXTRA)
    for i in range(rows // LANES):
        inverse = lax.rsqrt((tail[i : i + 1] + tail[2 + i : 3 + i]) * (1.0 / D) + 1e-6)
        scale_ref[pl.ds(i * LANES, LANES), :] = jnp.broadcast_to(inverse, (LANES, LANES)).T
    streams = [stream(refs, g * rows, scale_ref, filt_ref, 1 + g, ext_ref.at[g]) for g in range(2)]
    head_ref[...] = jnp.zeros_like(head_ref)
    for g in range(2):
        head_ref[2 * g : 2 * g + 2] = streams[g][:2]
    signal = streams[0] * streams[1]
    row = lax.broadcasted_iota(jnp.int32, (rows, LANES), 0)
    sig_ref[...] = jnp.where(row < 2, 0.0, signal)
    wire_ref[HEAD:] = jnp.zeros((WIRE - HEAD, LANES), F32)
    for i, (g, at) in enumerate(((0, 0), (1, 0), (0, rows - 2), (1, rows - 2))):
        wire_ref[HEAD + 2 * i : HEAD + 2 * i + 2] = ext_ref[g, TILE + at : TILE + at + 2]
    gate = tail[4:6] * scale_ref[rows - 2 :]
    wire_ref[TAIL + 4 : TAIL + 6] = gate.astype(BF16).astype(F32)
    tiles = [[sig_ref[pl.ds(q * SUB + TILE * k, TILE), :] for k in range(STEPS)] for q in range(subs)]
    for m in range(MODES):
        real = [tiles[q][STEPS - 1] for q in range(subs)]
        imag = [None] * subs
        for k in range(STEPS - 1):
            by = [p8_ref[STEPS - 1 - k, c, m : m + 1, :] for c in range(2)]
            for q in range(subs):
                real[q] = real[q] + by[0] * tiles[q][k]
                term = by[1] * tiles[q][k]
                imag[q] = term if k == 0 else imag[q] + term
        for q in range(subs):
            turned = cmul((real[q], imag[q]), (r7_ref[m, 0], r7_ref[m, 1]))
            for c in range(2):
                u_ref[q, c, m : m + 1, :] = jnp.sum(turned[c], axis=0, keepdims=True)
    state = (jnp.zeros((MODES, LANES), F32),) * 2
    step = (p64_ref[1, 0], p64_ref[1, 1])
    for q in range(subs):
        for c in range(2):
            carry_ref[q, c] = state[c]
        state = cmul(state, step)
        state = (state[0] + u_ref[q, 0], state[1] + u_ref[q, 1])
    for c in range(2):
        wire_ref[MODES * c : MODES * (c + 1)] = state[c]
    wire = wire_ref[...].astype(send_ref.dtype)
    for i in range(LOW):
        send_ref[i] = wire


def edges(filt_ref, first, rim):
    def stream(g, own, old):
        taps = [filt_ref[3 * g + j : 3 * g + j + 1] for j in range(3)]
        return (
            taps[0] * own[0] + taps[1] * old[1] + taps[2] * old[0],
            taps[0] * own[1] + taps[1] * own[0] + taps[2] * old[1],
        )

    keys = stream(1, first[:2], rim[:2])
    values = stream(2, first[2:], rim[2:4])
    return keys[0] * values[0], keys[1] * values[1]


def lines(ref, at, count):
    return [ref[at + i : at + i + 1] for i in range(count)]


def impulses(plane_ref, at, pair):
    return [plane_ref[at, c] * pair[0] + plane_ref[at + 1, c] * pair[1] for c in range(2)]


def gathered(got_ref, wide_ref, plane_ref, at, filt_ref, tables, alone):
    zero = jnp.zeros((MODES, LANES), F32)
    sums = [[zero, zero] for _ in tables]
    for i in range(got_ref.shape[0]):
        wide_ref[i] = got_ref[i].astype(F32)
        value = [wide_ref[i, 0:MODES], wide_ref[i, MODES:HEAD]]
        if i or alone:
            rim = lines(wide_ref.at[i - 1], TAIL, 4) if i else [0.0] * 4
            extra = impulses(plane_ref, at, edges(filt_ref, lines(wide_ref.at[i], HEAD, 4), rim))
            value = [value[0] + extra[0], value[1] + extra[1]]
        for total, table_ref in zip(sums, tables):
            term = cmul(value, (table_ref[i, 0], table_ref[i, 1]))
            total[0], total[1] = total[0] + term[0], total[1] + term[1]
    return sums


def gate_kernel(a_ref, b_ref, c_ref, d_ref, scale_ref, filt_ref, gate_ref, ext_ref):
    gate_ref[...] = stream((a_ref, b_ref, c_ref, d_ref), 0, scale_ref, filt_ref, 0, ext_ref)


def plane_kernel(got_ref, mine_tab_ref, all_tab_ref, plane_ref, filt_ref, mine_ref, rim_ref, send_ref, wide_ref, wire_ref):
    mine, total = gathered(got_ref, wide_ref, plane_ref, 3, filt_ref, (mine_tab_ref, all_tab_ref), False)
    place = lax.rem(lax.axis_index("seq"), LOW)
    near = wide_ref[jnp.maximum(place - 1, 0), TAIL : TAIL + TILE]
    rim_ref[0] = jnp.where(place > 0, near, 0.0)
    rim_ref[1] = wide_ref[0, HEAD : HEAD + TILE]
    for c in range(2):
        mine_ref[c] = mine[c]
        wire_ref[c * MODES : (c + 1) * MODES] = total[c]
    wire_ref[HEAD:TAIL] = wide_ref[0, HEAD:TAIL]
    wire_ref[TAIL:] = wide_ref[LOW - 1, TAIL:]
    wire = wire_ref[...].astype(send_ref.dtype)
    for i in range(PLANES):
        send_ref[i] = wire


def final_kernel(
    got_ref, far_tab_ref, rim_ref, plane_ref, filt_ref, mine_ref, carry_ref, p64_ref, p8_ref, gt_ref, gate_ref, local_ref,
    head_ref, skip_ref, before_ref, out_ref, wide_ref, e_ref, y_ref, fix_ref,
):
    rows = gate_ref.shape[0]
    subs = rows // SUB
    (far,) = gathered(got_ref, wide_ref, plane_ref, 5, filt_ref, (far_tab_ref,), True)
    far = cmul(far, (plane_ref[0, 0], plane_ref[0, 1]))
    block = lax.axis_index("seq")
    place, plane = lax.rem(block, LOW), lax.div(block, LOW)
    old = jnp.where(plane > 0, wide_ref[jnp.maximum(plane - 1, 0), TAIL : TAIL + TILE], 0.0)
    extra = impulses(plane_ref, 3, edges(filt_ref, lines(rim_ref.at[1], 0, 4), [old[i : i + 1] for i in range(4)]))
    near = cmul(extra, (plane_ref[1, 0], plane_ref[1, 1]))
    rim = rim_ref[0] + jnp.where(place > 0, 0.0, old)
    old = {1: (rim[0:1], rim[1:2]), 2: (rim[2:3], rim[3:4]), 0: (rim[4:5], rim[5:6])}
    late = {}
    for g in range(3):
        taps = [filt_ref[3 * g + j : 3 * g + j + 1] for j in range(3)]
        late[g] = (taps[1] * old[g][1] + taps[2] * old[g][0], taps[2] * old[g][1])
    pair = [
        (head_ref[i : i + 1] + late[1][i]) * (head_ref[2 + i : 3 + i] + late[2][i]) for i in range(2)
    ]
    own = impulses(plane_ref, 7, pair)
    enter = [mine_ref[c] + near[c] + far[c] + own[c] for c in range(2)]
    fix_ref[...] = jnp.zeros_like(fix_ref)
    for i in range(2):
        fix_ref[0, i : i + 1] = late[0][i]
        fix_ref[1, i : i + 1] = skip_ref[...] * pair[i]
    fix_ref[1, 0:1] -= before_ref[...] * pair[1]
    for q in range(subs):
        moved = cmul(enter, (p64_ref[q, 0], p64_ref[q, 1])) if q else enter
        for c in range(2):
            e_ref[q, c] = moved[c] + carry_ref[q, c]
    sums = [[None] * STEPS for _ in range(subs)]
    for m in range(MODES):
        table = (gt_ref[m, 0], gt_ref[m, 1])
        value = [cmul(table, (e_ref[q, 0, m : m + 1, :], e_ref[q, 1, m : m + 1, :])) for q in range(subs)]
        for k in range(STEPS):
            if k:
                by = [p8_ref[k, c, m : m + 1, :] for c in range(2)]
            for q in range(subs):
                term = by[0] * value[q][0] - by[1] * value[q][1] if k else value[q][0]
                sums[q][k] = term if m == 0 else sums[q][k] + term
    for q in range(subs):
        for k in range(STEPS):
            at = pl.ds(q * SUB + TILE * k, TILE)
            gate, conv = gate_ref[at, :], local_ref[at, :] + sums[q][k]
            if q == 0 and k == 0:
                gate, conv = gate + fix_ref[0], conv + fix_ref[1]
            y_ref[at, :] = gate * conv
    out_ref[...] = y_ref[...].T.astype(BF16)


def body(tokens, norm_gain, in_weight, short_filter, decay_reach, mode_freq, residues, skip_gain):
    rows, cols = tokens.shape
    fsdp = lax.axis_size("fsdp")
    state = shape(2, MODES, LANES)

    packed = 2 * rows + EXTRA
    weight = jnp.transpose(in_weight, (1, 0, 2))
    block = shape(packed, LANES, dtype=BF16)

    def exchange(own, *parts):
        sent = {
            d: lax.ppermute(parts[d - 1], "fsdp", [(i, (i + d) % fsdp) for i in range(fsdp)]) for d in (2, 1, 3)
        }
        return own, sent[1], sent[2], sent[3]

    products = call(
        project_kernel,
        (shape(packed, LANES), block, block, block, shape(rows, LANES), *[shape(rows, LANES, dtype=BF16)] * 3),
        (tokens, pltpu.with_memory_space_constraint(norm_gain[None], pltpu.HBM), weight),
        [
            pltpu.VMEM((rows, cols), BF16),
            pltpu.VMEM((1, cols), F32),
            pltpu.VMEM((3, cols, 4 * LANES), BF16),
            pltpu.VMEM((rows, cols), BF16),
            pltpu.VMEM((rows, LANES), F32),
            pltpu.VMEM((EXTRA, LANES), F32),
            pltpu.VMEM((rows, 4 * LANES), F32),
            pltpu.SemaphoreType.DMA((5,)),
            pltpu.SemaphoreType.DMA((3,)),
        ],
        limit=52 << 20,
        flops=2 * rows * cols * 12 * LANES,
        places=[HBM] * 3,
    )
    pair = exchange(*products[:4])
    gates = exchange(*products[4:])
    p8, r7, gt, p64, mine_tab, all_tab, far_tab, plane_tab, taps, before = call(
        table_kernel,
        (
            shape(STEPS, 2, MODES, LANES),
            shape(MODES, 2, TILE, LANES),
            shape(MODES, 2, TILE, LANES),
            shape(4, 2, MODES, LANES),
            shape(LOW, 2, MODES, LANES),
            shape(LOW, 2, MODES, LANES),
            shape(PLANES, 2, MODES, LANES),
            shape(9, 2, MODES, LANES),
            shape(SUB, LANES),
            shape(1, LANES),
        ),
        (decay_reach.T, mode_freq.T, residues.T),
        [pltpu.VMEM((2 * LOW, 2, MODES, LANES), F32)],
        flops=1 << 27,
    )
    filt = jnp.transpose(short_filter, (1, 2, 0)).reshape(9, LANES)
    skip = skip_gain[None]
    wire = shape(LOW, WIRE, LANES, dtype=BF16)
    scale, signal, carry, send, head = call(
        signal_kernel,
        (shape(rows, LANES), shape(rows, LANES), shape(4, 2, MODES, LANES), wire, shape(TILE, LANES)),
        (*pair, filt, p8, r7, p64),
        [
            pltpu.VMEM((2, TILE + rows, LANES), F32),
            pltpu.VMEM((4, 2, MODES, LANES), F32),
            pltpu.VMEM((WIRE, LANES), F32),
        ],
        flops=1 << 27,
    )
    plane = [[LOW * g + j for j in range(LOW)] for g in range(PLANES)]
    got = lax.all_to_all(send, "seq", 0, 0, axis_index_groups=plane)
    mine, rim, send = call(
        plane_kernel,
        (state, shape(2, TILE, LANES), wire),
        (got, mine_tab, all_tab, plane_tab, filt),
        [pltpu.VMEM((LOW, WIRE, LANES), F32), pltpu.VMEM((WIRE, LANES), F32)],
        flops=1 << 24,
    )
    local_part = call(
        local_kernel,
        shape(rows, LANES),
        (signal, skip, taps, rim),
        [pltpu.VMEM((TILE + SUB, LANES), F32)],
        flops=1 << 27,
    )
    gate = call(
        gate_kernel,
        shape(rows, LANES),
        (*gates, scale, filt),
        [pltpu.VMEM((TILE + rows, LANES), F32)],
        flops=1 << 24,
    )
    line = [[LOW * j + g for j in range(PLANES)] for g in range(LOW)]
    got = lax.all_to_all(send, "seq", 0, 0, axis_index_groups=line)
    return call(
        final_kernel,
        shape(LANES, rows, dtype=BF16),
        (got, far_tab, rim, plane_tab, filt, mine, carry, p64, p8, gt, gate, local_part, head, skip, before),
        [
            pltpu.VMEM((PLANES, WIRE, LANES), F32),
            pltpu.VMEM((4, 2, MODES, LANES), F32),
            pltpu.VMEM((rows, LANES), F32),
            pltpu.VMEM((2, TILE, LANES), F32),
        ],
        flops=1 << 27,
    )


def solution(mesh):
    placed = (
        P("seq", "fsdp"),
        P("fsdp"),
        P("fsdp", None, None),
        P("fsdp", None, None),
        P("fsdp", None),
        P("fsdp", None),
        P("fsdp", None),
        P("fsdp"),
    )
    return jax.shard_map(
        body, mesh=mesh, in_specs=placed, out_specs=P("fsdp", "seq"), check_vma=False
    )
```

```python
import math

import jax
import jax.numpy as jnp
from jax import lax
from jax.experimental import pallas as pl
from jax.experimental.pallas import tpu as pltpu
from jax.sharding import PartitionSpec as P

F32 = jnp.float32
BF16 = jnp.bfloat16
D = 8192
MODES = 16
LANES = 128
TILE = 8
SUB = 64
STEPS = SUB // TILE
LOW = 8
PLANES = 8
HEAD = 2 * MODES
TAIL = HEAD + 4
EXTRA = 16
WIRE = 48
VMEM = pl.BlockSpec(memory_space=pltpu.VMEM)
HBM = pl.BlockSpec(memory_space=pltpu.HBM)


def call(kernel, out_shape, operands, scratch=(), limit=16 << 20, flops=0, places=None):
    moved = sum(math.prod(v.shape) * v.dtype.itemsize for v in (*operands, *jax.tree.leaves(out_shape)))
    return pl.pallas_call(
        kernel,
        out_shape=out_shape,
        in_specs=places or [VMEM] * len(operands),
        out_specs=jax.tree.map(lambda _: VMEM, out_shape),
        scratch_shapes=list(scratch),
        compiler_params=pltpu.CompilerParams(vmem_limit_bytes=limit),
        cost_estimate=pl.CostEstimate(flops=flops, bytes_accessed=moved, transcendentals=0),
    )(*operands)


def shape(*dims, dtype=F32):
    return jax.ShapeDtypeStruct(dims, dtype)


def cmul(a, b):
    return a[0] * b[0] - a[1] * b[1], a[0] * b[1] + a[1] * b[0]


def turn(angle):
    cycles = jnp.floor(angle * (0.5 / math.pi) + 0.5)
    rest = angle - cycles * 6.28125
    rest = rest - cycles * 1.93500518798828125e-3
    rest = rest - cycles * 3.0199159819e-7
    return jnp.cos(rest), jnp.sin(rest)


def table_kernel(
    reach_ref, freq_ref, res_ref, p8_ref, r7_ref, gt_ref, p64_ref, mine_ref, all_ref, far_ref, plane_ref, h_ref, before_ref, power_ref
):
    rate = 1.0 / reach_ref[...]
    freq = freq_ref[...]
    gain = res_ref[...] * jnp.sqrt(2.0 * rate)
    block = lax.axis_index("seq")
    place = lax.rem(block, LOW)
    plane = lax.div(block, LOW)

    def power(n):
        size = jnp.exp(-rate * n)
        cosine, sine = turn(freq * n)
        return size * cosine, size * sine

    one = (jnp.ones_like(rate), jnp.zeros_like(rate))

    def chain(base, count):
        values = [one]
        for _ in range(count - 1):
            values.append(cmul(values[-1], base))
        return values

    ones = chain(power(1.0), TILE + 1)
    for j in range(TILE):
        for c in range(2):
            r7_ref[:, c, j, :] = ones[TILE - 1 - j][c]
            gt_ref[:, c, j, :] = gain * ones[j + 1][c]
    eights = chain(power(8.0), STEPS)
    for k in range(STEPS):
        for c in range(2):
            p8_ref[k, c] = eights[k][c]
    for q, value in enumerate(chain(power(float(SUB)), 4)):
        for c in range(2):
            p64_ref[q, c] = value[c]
    blocks = chain(power(256.0), LOW)
    for k, value in enumerate(blocks):
        for c in range(2):
            power_ref[k, c] = jnp.zeros_like(rate)
            power_ref[LOW + k, c] = value[c]
    for i in range(LOW):
        for c in range(2):
            mine_ref[i, c] = power_ref[LOW - 1 - i + place, c]
            all_ref[i, c] = blocks[LOW - 1 - i][c]
    unit, far = power(1.0), power(2048.0)
    size = jnp.exp(2.0 * rate)
    back = (size * unit[0], -size * unit[1])
    twice = cmul(back, back)
    last = cmul(blocks[1], back)
    earlier = cmul(last, back)
    rows = (
        (power_ref[LOW + place, 0], power_ref[LOW + place, 1]),
        (power_ref[LOW - 1 + place, 0], power_ref[LOW - 1 + place, 1]),
        far,
        last,
        earlier,
        cmul(last, blocks[LOW - 1]),
        cmul(earlier, blocks[LOW - 1]),
        back,
        twice,
    )
    for i, value in enumerate(rows):
        for c in range(2):
            plane_ref[i, c] = value[c]
    for k, value in enumerate(chain(far, PLANES)):
        for c in range(2):
            power_ref[LOW + k, c] = value[c]
    for i in range(PLANES):
        for c in range(2):
            far_ref[i, c] = power_ref[LOW - 1 - i + plane, c]
    before_ref[...] = jnp.sum(gain * back[0], axis=0, keepdims=True)
    taps = [jnp.zeros((TILE, LANES), F32) for _ in range(STEPS)]
    row = lax.broadcasted_iota(jnp.int32, (TILE, LANES), 0)
    for m in range(MODES):
        real = jnp.where(row == 0, gain[m : m + 1], pltpu.roll(gt_ref[m, 0], 1, 0))
        imag = jnp.where(row == 0, 0.0, pltpu.roll(gt_ref[m, 1], 1, 0))
        for k in range(STEPS):
            taps[k] = taps[k] + (eights[k][0][m : m + 1] * real - eights[k][1][m : m + 1] * imag)
    for k in range(STEPS):
        h_ref[TILE * k : TILE * k + TILE] = taps[k]


def project_kernel(
    tok_hbm, gain_hbm, w_hbm, own_ref, one_ref, two_ref, three_ref, own_gate, one_gate, two_gate, three_gate,
    tok_ref, gain_ref, w_ref, xg_ref, acc_ref, ext_ref, got_ref, sems, w_sems,
):
    rows, cols = tok_ref.shape
    outs = (own_ref, one_ref, two_ref, three_ref)
    gates = (own_gate, one_gate, two_gate, three_gate)
    pieces = 4
    span = rows // pieces
    gain_copy = pltpu.make_async_copy(gain_hbm, gain_ref, sems.at[0])
    gain_copy.start()
    tok_copies = []
    for i in range(pieces):
        at = pl.ds(i * span, span)
        tok_copies.append(pltpu.make_async_copy(tok_hbm.at[at], tok_ref.at[at], sems.at[1 + i]))
        tok_copies[-1].start(priority=i % 2)
    w_copies = [pltpu.make_async_copy(w_hbm.at[(g + 1) % 3], w_ref.at[g], w_sems.at[g]) for g in range(3)]
    w_copies[0].start(priority=0)
    w_copies[1].start(priority=1)
    gain_copy.wait()
    gain = gain_ref[...]
    for i in range(pieces):
        tok_copies[i].wait()
        if i == 1:
            w_copies[2].start(priority=0)
        for lo in range(i * span, (i + 1) * span, 32):
            x = tok_ref[pl.ds(lo, 32), :].astype(F32)
            xg_ref[pl.ds(lo, 32), :] = (x * gain).astype(BF16)
    me = lax.axis_index("fsdp")
    for g in range(3):
        w_copies[g].wait()
        got_ref[...] = jnp.dot(xg_ref[...], w_ref[g], preferred_element_type=F32)
        if g == 0:
            for lo in range(0, rows, 32):
                x = tok_ref[pl.ds(lo, 32), :].astype(F32)
                sq = x * x
                acc_ref[pl.ds(lo, 32), :] = sum(sq[:, j : j + LANES] for j in range(0, cols, LANES))
        for d in range(4):
            at = pl.ds(pl.multiple_of(lax.rem(me + d, 4) * LANES, LANES), LANES)
            if g < 2:
                outs[d][g * rows : (g + 1) * rows] = got_ref[:, at].astype(outs[d].dtype)
            else:
                gates[d][...] = got_ref[:, at].astype(gates[d].dtype)
    acc = acc_ref[...]
    high = acc.astype(BF16)
    mid = (acc - high.astype(F32)).astype(BF16)
    ones = jnp.ones((16, LANES), BF16)
    dims = (((1,), (1,)), ((), ()))
    total = (
        lax.dot_general(ones, high, dims, preferred_element_type=F32)
        + lax.dot_general(ones, mid, dims, preferred_element_type=F32)
    )[:1]
    ext_ref[...] = jnp.zeros_like(ext_ref)
    for i in range(rows // LANES):
        value = total[:, i * LANES : (i + 1) * LANES]
        high = value.astype(BF16).astype(F32)
        ext_ref[i : i + 1] = high
        ext_ref[2 + i : 3 + i] = value - high
    for d in range(4):
        at = pl.ds(pl.multiple_of(lax.rem(me + d, 4) * LANES, LANES), LANES)
        ext_ref[4:6] = got_ref[rows - 2 : rows, at]
        outs[d][2 * rows :] = ext_ref[...].astype(outs[d].dtype)


def local_kernel(sig_ref, skip_ref, h_ref, _, out_ref, pad_ref):
    pad_ref[0:TILE] = jnp.zeros((TILE, LANES), F32)
    for q in range(sig_ref.shape[0] // SUB):
        pad_ref[TILE:] = sig_ref[pl.ds(q * SUB, SUB), :]
        sums = [skip_ref[...] * pad_ref[pl.ds(TILE + TILE * i, TILE), :] for i in range(STEPS)]
        for b in range(TILE):
            moved = [pad_ref[pl.ds(TILE + TILE * i - b, TILE), :] for i in range(STEPS)]
            for a in range(STEPS):
                tap = h_ref[TILE * a + b : TILE * a + b + 1, :]
                for i in range(a, STEPS):
                    sums[i] = sums[i] + tap * moved[i - a]
        for i in range(STEPS):
            out_ref[pl.ds(q * SUB + TILE * i, TILE), :] = sums[i]


def summed(refs, lo, n):
    at = pl.ds(lo, n)
    return refs[0][at, :] + (refs[1][at, :].astype(F32) + refs[2][at, :].astype(F32) + refs[3][at, :].astype(F32))


def stream(refs, lo, scale_ref, filt_ref, g, ext_ref):
    rows = scale_ref.shape[0]
    ext_ref[0:TILE] = jnp.zeros((TILE, LANES), F32)
    for i in range(0, rows, LANES):
        value = summed(refs, lo + i, LANES) * scale_ref[pl.ds(i, LANES), :]
        ext_ref[pl.ds(TILE + i, LANES), :] = value.astype(BF16).astype(F32)
    taps = [filt_ref[3 * g + j : 3 * g + j + 1] for j in range(3)]
    return (
        taps[0] * ext_ref[pl.ds(TILE, rows), :]
        + taps[1] * ext_ref[pl.ds(TILE - 1, rows), :]
        + taps[2] * ext_ref[pl.ds(TILE - 2, rows), :]
    )


def signal_kernel(
    a_ref, b_ref, c_ref, d_ref, filt_ref, p8_ref, r7_ref, p64_ref,
    scale_ref, sig_ref, carry_ref, send_ref, head_ref, ext_ref, u_ref, wire_ref,
):
    rows = sig_ref.shape[0]
    subs = rows // SUB
    refs = (a_ref, b_ref, c_ref, d_ref)
    tail = summed(refs, 2 * rows, EXTRA)
    for i in range(rows // LANES):
        inverse = lax.rsqrt((tail[i : i + 1] + tail[2 + i : 3 + i]) * (1.0 / D) + 1e-6)
        scale_ref[pl.ds(i * LANES, LANES), :] = jnp.broadcast_to(inverse, (LANES, LANES)).T
    streams = [stream(refs, g * rows, scale_ref, filt_ref, 1 + g, ext_ref.at[g]) for g in range(2)]
    head_ref[...] = jnp.zeros_like(head_ref)
    for g in range(2):
        head_ref[2 * g : 2 * g + 2] = streams[g][:2]
    signal = streams[0] * streams[1]
    row = lax.broadcasted_iota(jnp.int32, (rows, LANES), 0)
    sig_ref[...] = jnp.where(row < 2, 0.0, signal)
    wire_ref[HEAD:] = jnp.zeros((WIRE - HEAD, LANES), F32)
    for i, (g, at) in enumerate(((0, 0), (1, 0), (0, rows - 2), (1, rows - 2))):
        wire_ref[HEAD + 2 * i : HEAD + 2 * i + 2] = ext_ref[g, TILE + at : TILE + at + 2]
    gate = tail[4:6] * scale_ref[rows - 2 :]
    wire_ref[TAIL + 4 : TAIL + 6] = gate.astype(BF16).astype(F32)
    tiles = [[sig_ref[pl.ds(q * SUB + TILE * k, TILE), :] for k in range(STEPS)] for q in range(subs)]
    for m in range(MODES):
        real = [tiles[q][STEPS - 1] for q in range(subs)]
        imag = [None] * subs
        for k in range(STEPS - 1):
            by = [p8_ref[STEPS - 1 - k, c, m : m + 1, :] for c in range(2)]
            for q in range(subs):
                real[q] = real[q] + by[0] * tiles[q][k]
                term = by[1] * tiles[q][k]
                imag[q] = term if k == 0 else imag[q] + term
        for q in range(subs):
            turned = cmul((real[q], imag[q]), (r7_ref[m, 0], r7_ref[m, 1]))
            for c in range(2):
                u_ref[q, c, m : m + 1, :] = jnp.sum(turned[c], axis=0, keepdims=True)
    state = (jnp.zeros((MODES, LANES), F32),) * 2
    step = (p64_ref[1, 0], p64_ref[1, 1])
    for q in range(subs):
        for c in range(2):
            carry_ref[q, c] = state[c]
        state = cmul(state, step)
        state = (state[0] + u_ref[q, 0], state[1] + u_ref[q, 1])
    for c in range(2):
        wire_ref[MODES * c : MODES * (c + 1)] = state[c]
    wire = wire_ref[...].astype(send_ref.dtype)
    for i in range(LOW):
        send_ref[i] = wire


def edges(filt_ref, first, rim):
    def stream(g, own, old):
        taps = [filt_ref[3 * g + j : 3 * g + j + 1] for j in range(3)]
        return (
            taps[0] * own[0] + taps[1] * old[1] + taps[2] * old[0],
            taps[0] * own[1] + taps[1] * own[0] + taps[2] * old[1],
        )

    keys = stream(1, first[:2], rim[:2])
    values = stream(2, first[2:], rim[2:4])
    return keys[0] * values[0], keys[1] * values[1]


def lines(ref, at, count):
    return [ref[at + i : at + i + 1] for i in range(count)]


def impulses(plane_ref, at, pair):
    return [plane_ref[at, c] * pair[0] + plane_ref[at + 1, c] * pair[1] for c in range(2)]


def gathered(got_ref, wide_ref, plane_ref, at, filt_ref, tables, alone):
    zero = jnp.zeros((MODES, LANES), F32)
    sums = [[zero, zero] for _ in tables]
    for i in range(got_ref.shape[0]):
        wide_ref[i] = got_ref[i].astype(F32)
        value = [wide_ref[i, 0:MODES], wide_ref[i, MODES:HEAD]]
        if i or alone:
            rim = lines(wide_ref.at[i - 1], TAIL, 4) if i else [0.0] * 4
            extra = impulses(plane_ref, at, edges(filt_ref, lines(wide_ref.at[i], HEAD, 4), rim))
            value = [value[0] + extra[0], value[1] + extra[1]]
        for total, table_ref in zip(sums, tables):
            term = cmul(value, (table_ref[i, 0], table_ref[i, 1]))
            total[0], total[1] = total[0] + term[0], total[1] + term[1]
    return sums


def gate_kernel(a_ref, b_ref, c_ref, d_ref, scale_ref, filt_ref, _, gate_ref, ext_ref):
    gate_ref[...] = stream((a_ref, b_ref, c_ref, d_ref), 0, scale_ref, filt_ref, 0, ext_ref)


def plane_kernel(got_ref, mine_tab_ref, all_tab_ref, plane_ref, filt_ref, mine_ref, rim_ref, send_ref, wide_ref, wire_ref):
    mine, total = gathered(got_ref, wide_ref, plane_ref, 3, filt_ref, (mine_tab_ref, all_tab_ref), False)
    place = lax.rem(lax.axis_index("seq"), LOW)
    near = wide_ref[jnp.maximum(place - 1, 0), TAIL : TAIL + TILE]
    rim_ref[0] = jnp.where(place > 0, near, 0.0)
    rim_ref[1] = wide_ref[0, HEAD : HEAD + TILE]
    for c in range(2):
        mine_ref[c] = mine[c]
        wire_ref[c * MODES : (c + 1) * MODES] = total[c]
    wire_ref[HEAD:TAIL] = wide_ref[0, HEAD:TAIL]
    wire_ref[TAIL:] = wide_ref[LOW - 1, TAIL:]
    wire = wire_ref[...].astype(send_ref.dtype)
    for i in range(PLANES):
        send_ref[i] = wire


def final_kernel(
    got_ref, far_tab_ref, rim_ref, plane_ref, filt_ref, mine_ref, carry_ref, p64_ref, p8_ref, gt_ref, gate_ref, local_ref,
    head_ref, skip_ref, before_ref, out_ref, wide_ref, e_ref, y_ref, fix_ref,
):
    rows = gate_ref.shape[0]
    subs = rows // SUB
    (far,) = gathered(got_ref, wide_ref, plane_ref, 5, filt_ref, (far_tab_ref,), True)
    far = cmul(far, (plane_ref[0, 0], plane_ref[0, 1]))
    block = lax.axis_index("seq")
    place, plane = lax.rem(block, LOW), lax.div(block, LOW)
    old = jnp.where(plane > 0, wide_ref[jnp.maximum(plane - 1, 0), TAIL : TAIL + TILE], 0.0)
    extra = impulses(plane_ref, 3, edges(filt_ref, lines(rim_ref.at[1], 0, 4), [old[i : i + 1] for i in range(4)]))
    near = cmul(extra, (plane_ref[1, 0], plane_ref[1, 1]))
    rim = rim_ref[0] + jnp.where(place > 0, 0.0, old)
    old = {1: (rim[0:1], rim[1:2]), 2: (rim[2:3], rim[3:4]), 0: (rim[4:5], rim[5:6])}
    late = {}
    for g in range(3):
        taps = [filt_ref[3 * g + j : 3 * g + j + 1] for j in range(3)]
        late[g] = (taps[1] * old[g][1] + taps[2] * old[g][0], taps[2] * old[g][1])
    pair = [
        (head_ref[i : i + 1] + late[1][i]) * (head_ref[2 + i : 3 + i] + late[2][i]) for i in range(2)
    ]
    own = impulses(plane_ref, 7, pair)
    enter = [mine_ref[c] + near[c] + far[c] + own[c] for c in range(2)]
    fix_ref[...] = jnp.zeros_like(fix_ref)
    for i in range(2):
        fix_ref[0, i : i + 1] = late[0][i]
        fix_ref[1, i : i + 1] = skip_ref[...] * pair[i]
    fix_ref[1, 0:1] -= before_ref[...] * pair[1]
    for q in range(subs):
        moved = cmul(enter, (p64_ref[q, 0], p64_ref[q, 1])) if q else enter
        for c in range(2):
            e_ref[q, c] = moved[c] + carry_ref[q, c]
    sums = [[None] * STEPS for _ in range(subs)]
    for m in range(MODES):
        table = (gt_ref[m, 0], gt_ref[m, 1])
        value = [cmul(table, (e_ref[q, 0, m : m + 1, :], e_ref[q, 1, m : m + 1, :])) for q in range(subs)]
        for k in range(STEPS):
            if k:
                by = [p8_ref[k, c, m : m + 1, :] for c in range(2)]
            for q in range(subs):
                term = by[0] * value[q][0] - by[1] * value[q][1] if k else value[q][0]
                sums[q][k] = term if m == 0 else sums[q][k] + term
    for q in range(subs):
        for k in range(STEPS):
            at = pl.ds(q * SUB + TILE * k, TILE)
            gate, conv = gate_ref[at, :], local_ref[at, :] + sums[q][k]
            if q == 0 and k == 0:
                gate, conv = gate + fix_ref[0], conv + fix_ref[1]
            y_ref[at, :] = gate * conv
    out_ref[...] = y_ref[...].T.astype(BF16)


def body(tokens, norm_gain, in_weight, short_filter, decay_reach, mode_freq, residues, skip_gain):
    rows, cols = tokens.shape
    fsdp = lax.axis_size("fsdp")
    state = shape(2, MODES, LANES)

    packed = 2 * rows + EXTRA
    weight = jnp.transpose(in_weight, (1, 0, 2))
    block = shape(packed, LANES, dtype=BF16)

    def exchange(own, *parts):
        sent = {
            d: lax.ppermute(parts[d - 1], "fsdp", [(i, (i + d) % fsdp) for i in range(fsdp)]) for d in (2, 1, 3)
        }
        return own, sent[1], sent[2], sent[3]

    products = call(
        project_kernel,
        (shape(packed, LANES), block, block, block, shape(rows, LANES), *[shape(rows, LANES, dtype=BF16)] * 3),
        (tokens, pltpu.with_memory_space_constraint(norm_gain[None], pltpu.HBM), weight),
        [
            pltpu.VMEM((rows, cols), BF16),
            pltpu.VMEM((1, cols), F32),
            pltpu.VMEM((3, cols, 4 * LANES), BF16),
            pltpu.VMEM((rows, cols), BF16),
            pltpu.VMEM((rows, LANES), F32),
            pltpu.VMEM((EXTRA, LANES), F32),
            pltpu.VMEM((rows, 4 * LANES), F32),
            pltpu.SemaphoreType.DMA((5,)),
            pltpu.SemaphoreType.DMA((3,)),
        ],
        limit=52 << 20,
        flops=2 * rows * cols * 12 * LANES,
        places=[HBM] * 3,
    )
    pair = exchange(*products[:4])
    gates = exchange(*products[4:])
    p8, r7, gt, p64, mine_tab, all_tab, far_tab, plane_tab, taps, before = call(
        table_kernel,
        (
            shape(STEPS, 2, MODES, LANES),
            shape(MODES, 2, TILE, LANES),
            shape(MODES, 2, TILE, LANES),
            shape(4, 2, MODES, LANES),
            shape(LOW, 2, MODES, LANES),
            shape(LOW, 2, MODES, LANES),
            shape(PLANES, 2, MODES, LANES),
            shape(9, 2, MODES, LANES),
            shape(SUB, LANES),
            shape(1, LANES),
        ),
        (decay_reach.T, mode_freq.T, residues.T),
        [pltpu.VMEM((2 * LOW, 2, MODES, LANES), F32)],
        flops=1 << 27,
    )
    filt = jnp.transpose(short_filter, (1, 2, 0)).reshape(9, LANES)
    skip = skip_gain[None]
    wire = shape(LOW, WIRE, LANES, dtype=BF16)
    scale, signal, carry, send, head = call(
        signal_kernel,
        (shape(rows, LANES), shape(rows, LANES), shape(4, 2, MODES, LANES), wire, shape(TILE, LANES)),
        (*pair, filt, p8, r7, p64),
        [
            pltpu.VMEM((2, TILE + rows, LANES), F32),
            pltpu.VMEM((4, 2, MODES, LANES), F32),
            pltpu.VMEM((WIRE, LANES), F32),
        ],
        flops=1 << 27,
    )
    plane = [[LOW * g + j for j in range(LOW)] for g in range(PLANES)]
    got = lax.all_to_all(send, "seq", 0, 0, axis_index_groups=plane)
    mine, rim, send = call(
        plane_kernel,
        (state, shape(2, TILE, LANES), wire),
        (got, mine_tab, all_tab, plane_tab, filt),
        [pltpu.VMEM((LOW, WIRE, LANES), F32), pltpu.VMEM((WIRE, LANES), F32)],
        flops=1 << 24,
    )
    local_part = call(
        local_kernel,
        shape(rows, LANES),
        (signal, skip, taps, rim),
        [pltpu.VMEM((TILE + SUB, LANES), F32)],
        flops=1 << 27,
    )
    gate = call(
        gate_kernel,
        shape(rows, LANES),
        (*gates, scale, filt, local_part),
        [pltpu.VMEM((TILE + rows, LANES), F32)],
        flops=1 << 24,
    )
    line = [[LOW * j + g for j in range(PLANES)] for g in range(LOW)]
    got = lax.all_to_all(send, "seq", 0, 0, axis_index_groups=line)
    return call(
        final_kernel,
        shape(LANES, rows, dtype=BF16),
        (got, far_tab, rim, plane_tab, filt, mine, carry, p64, p8, gt, gate, local_part, head, skip, before),
        [
            pltpu.VMEM((PLANES, WIRE, LANES), F32),
            pltpu.VMEM((4, 2, MODES, LANES), F32),
            pltpu.VMEM((rows, LANES), F32),
            pltpu.VMEM((2, TILE, LANES), F32),
        ],
        flops=1 << 27,
    )


def solution(mesh):
    placed = (
        P("seq", "fsdp"),
        P("fsdp"),
        P("fsdp", None, None),
        P("fsdp", None, None),
        P("fsdp", None),
        P("fsdp", None),
        P("fsdp", None),
        P("fsdp"),
    )
    return jax.shard_map(
        body, mesh=mesh, in_specs=placed, out_specs=P("fsdp", "seq"), check_vma=False
    )
```

```python
import math

import jax
import jax.numpy as jnp
from jax import lax
from jax.experimental import pallas as pl
from jax.experimental.pallas import tpu as pltpu
from jax.sharding import PartitionSpec as P

F32 = jnp.float32
BF16 = jnp.bfloat16
D = 8192
MODES = 16
LANES = 128
TILE = 8
SUB = 64
STEPS = SUB // TILE
LOW = 8
PLANES = 8
HEAD = 2 * MODES
TAIL = HEAD + 4
EXTRA = 16
WIRE = 48
VMEM = pl.BlockSpec(memory_space=pltpu.VMEM)
HBM = pl.BlockSpec(memory_space=pltpu.HBM)


def call(kernel, out_shape, operands, scratch=(), limit=16 << 20, flops=0, places=None):
    moved = sum(math.prod(v.shape) * v.dtype.itemsize for v in (*operands, *jax.tree.leaves(out_shape)))
    return pl.pallas_call(
        kernel,
        out_shape=out_shape,
        in_specs=places or [VMEM] * len(operands),
        out_specs=jax.tree.map(lambda _: VMEM, out_shape),
        scratch_shapes=list(scratch),
        compiler_params=pltpu.CompilerParams(vmem_limit_bytes=limit),
        cost_estimate=pl.CostEstimate(flops=flops, bytes_accessed=moved, transcendentals=0),
    )(*operands)


def shape(*dims, dtype=F32):
    return jax.ShapeDtypeStruct(dims, dtype)


def cmul(a, b):
    return a[0] * b[0] - a[1] * b[1], a[0] * b[1] + a[1] * b[0]


def turn(angle):
    cycles = jnp.floor(angle * (0.5 / math.pi) + 0.5)
    rest = angle - cycles * 6.28125
    rest = rest - cycles * 1.93500518798828125e-3
    rest = rest - cycles * 3.0199159819e-7
    return jnp.cos(rest), jnp.sin(rest)


def table_kernel(
    reach_ref, freq_ref, res_ref, p8_ref, r7_ref, gt_ref, p64_ref, mine_ref, all_ref, far_ref, plane_ref, h_ref, before_ref, power_ref
):
    rate = 1.0 / reach_ref[...]
    freq = freq_ref[...]
    gain = res_ref[...] * jnp.sqrt(2.0 * rate)
    block = lax.axis_index("seq")
    place = lax.rem(block, LOW)
    plane = lax.div(block, LOW)

    def power(n):
        size = jnp.exp(-rate * n)
        cosine, sine = turn(freq * n)
        return size * cosine, size * sine

    one = (jnp.ones_like(rate), jnp.zeros_like(rate))

    def chain(base, count):
        values = [one]
        for _ in range(count - 1):
            values.append(cmul(values[-1], base))
        return values

    ones = chain(power(1.0), TILE + 1)
    for j in range(TILE):
        for c in range(2):
            r7_ref[:, c, j, :] = ones[TILE - 1 - j][c]
            gt_ref[:, c, j, :] = gain * ones[j + 1][c]
    eights = chain(power(8.0), STEPS)
    for k in range(STEPS):
        for c in range(2):
            p8_ref[k, c] = eights[k][c]
    for q, value in enumerate(chain(power(float(SUB)), 4)):
        for c in range(2):
            p64_ref[q, c] = value[c]
    blocks = chain(power(256.0), LOW)
    for k, value in enumerate(blocks):
        for c in range(2):
            power_ref[k, c] = jnp.zeros_like(rate)
            power_ref[LOW + k, c] = value[c]
    for i in range(LOW):
        for c in range(2):
            mine_ref[i, c] = power_ref[LOW - 1 - i + place, c]
            all_ref[i, c] = blocks[LOW - 1 - i][c]
    unit, far = power(1.0), power(2048.0)
    size = jnp.exp(2.0 * rate)
    back = (size * unit[0], -size * unit[1])
    twice = cmul(back, back)
    last = cmul(blocks[1], back)
    earlier = cmul(last, back)
    rows = (
        (power_ref[LOW + place, 0], power_ref[LOW + place, 1]),
        (power_ref[LOW - 1 + place, 0], power_ref[LOW - 1 + place, 1]),
        far,
        last,
        earlier,
        cmul(last, blocks[LOW - 1]),
        cmul(earlier, blocks[LOW - 1]),
        back,
        twice,
    )
    for i, value in enumerate(rows):
        for c in range(2):
            plane_ref[i, c] = value[c]
    for k, value in enumerate(chain(far, PLANES)):
        for c in range(2):
            power_ref[LOW + k, c] = value[c]
    for i in range(PLANES):
        for c in range(2):
            far_ref[i, c] = power_ref[LOW - 1 - i + plane, c]
    before_ref[...] = jnp.sum(gain * back[0], axis=0, keepdims=True)
    taps = [jnp.zeros((TILE, LANES), F32) for _ in range(STEPS)]
    row = lax.broadcasted_iota(jnp.int32, (TILE, LANES), 0)
    for m in range(MODES):
        real = jnp.where(row == 0, gain[m : m + 1], pltpu.roll(gt_ref[m, 0], 1, 0))
        imag = jnp.where(row == 0, 0.0, pltpu.roll(gt_ref[m, 1], 1, 0))
        for k in range(STEPS):
            taps[k] = taps[k] + (eights[k][0][m : m + 1] * real - eights[k][1][m : m + 1] * imag)
    for k in range(STEPS):
        h_ref[TILE * k : TILE * k + TILE] = taps[k]


def project_kernel(
    tok_hbm, gain_hbm, w_hbm, own_ref, one_ref, two_ref, three_ref, own_gate, one_gate, two_gate, three_gate,
    tok_ref, gain_ref, w_ref, xg_ref, acc_ref, ext_ref, got_ref, sems, w_sems,
):
    rows, cols = tok_ref.shape
    outs = (own_ref, one_ref, two_ref, three_ref)
    gates = (own_gate, one_gate, two_gate, three_gate)
    pieces = 4
    span = rows // pieces
    gain_copy = pltpu.make_async_copy(gain_hbm, gain_ref, sems.at[0])
    gain_copy.start()
    tok_copies = []
    for i in range(pieces):
        at = pl.ds(i * span, span)
        tok_copies.append(pltpu.make_async_copy(tok_hbm.at[at], tok_ref.at[at], sems.at[1 + i]))
        tok_copies[-1].start(priority=i % 2)
    w_copies = [pltpu.make_async_copy(w_hbm.at[(g + 1) % 3], w_ref.at[g], w_sems.at[g]) for g in range(3)]
    w_copies[0].start(priority=0)
    w_copies[1].start(priority=1)
    gain_copy.wait()
    gain = gain_ref[...]
    for i in range(pieces):
        tok_copies[i].wait()
        if i == 1:
            w_copies[2].start(priority=0)
        for lo in range(i * span, (i + 1) * span, 32):
            x = tok_ref[pl.ds(lo, 32), :].astype(F32)
            xg_ref[pl.ds(lo, 32), :] = (x * gain).astype(BF16)
    me = lax.axis_index("fsdp")
    for g in range(3):
        w_copies[g].wait()
        got_ref[...] = jnp.dot(xg_ref[...], w_ref[g], preferred_element_type=F32)
        if g == 0:
            for lo in range(0, rows, 32):
                x = tok_ref[pl.ds(lo, 32), :].astype(F32)
                sq = x * x
                acc_ref[pl.ds(lo, 32), :] = sum(sq[:, j : j + LANES] for j in range(0, cols, LANES))
        for d in range(4):
            at = pl.ds(pl.multiple_of(lax.rem(me + d, 4) * LANES, LANES), LANES)
            if g < 2:
                outs[d][g * rows : (g + 1) * rows] = got_ref[:, at].astype(outs[d].dtype)
            else:
                gates[d][...] = got_ref[:, at].astype(gates[d].dtype)
    acc = acc_ref[...]
    high = acc.astype(BF16)
    mid = (acc - high.astype(F32)).astype(BF16)
    ones = jnp.ones((16, LANES), BF16)
    dims = (((1,), (1,)), ((), ()))
    total = (
        lax.dot_general(ones, high, dims, preferred_element_type=F32)
        + lax.dot_general(ones, mid, dims, preferred_element_type=F32)
    )[:1]
    ext_ref[...] = jnp.zeros_like(ext_ref)
    for i in range(rows // LANES):
        value = total[:, i * LANES : (i + 1) * LANES]
        high = value.astype(BF16).astype(F32)
        ext_ref[i : i + 1] = high
        ext_ref[2 + i : 3 + i] = value - high
    for d in range(4):
        at = pl.ds(pl.multiple_of(lax.rem(me + d, 4) * LANES, LANES), LANES)
        ext_ref[4:6] = got_ref[rows - 2 : rows, at]
        outs[d][2 * rows :] = ext_ref[...].astype(outs[d].dtype)


def local_kernel(sig_ref, skip_ref, h_ref, _, out_ref, pad_ref):
    pad_ref[0:TILE] = jnp.zeros((TILE, LANES), F32)
    for q in range(sig_ref.shape[0] // SUB):
        pad_ref[TILE:] = sig_ref[pl.ds(q * SUB, SUB), :]
        sums = [skip_ref[...] * pad_ref[pl.ds(TILE + TILE * i, TILE), :] for i in range(STEPS)]
        for b in range(TILE):
            moved = [pad_ref[pl.ds(TILE + TILE * i - b, TILE), :] for i in range(STEPS)]
            for a in range(STEPS):
                tap = h_ref[TILE * a + b : TILE * a + b + 1, :]
                for i in range(a, STEPS):
                    sums[i] = sums[i] + tap * moved[i - a]
        for i in range(STEPS):
            out_ref[pl.ds(q * SUB + TILE * i, TILE), :] = sums[i]


def summed(refs, lo, n):
    at = pl.ds(lo, n)
    return refs[0][at, :] + (refs[1][at, :].astype(F32) + refs[2][at, :].astype(F32) + refs[3][at, :].astype(F32))


def stream(refs, lo, scale_ref, filt_ref, g, ext_ref):
    rows = scale_ref.shape[0]
    ext_ref[0:TILE] = jnp.zeros((TILE, LANES), F32)
    for i in range(0, rows, LANES):
        value = summed(refs, lo + i, LANES) * scale_ref[pl.ds(i, LANES), :]
        ext_ref[pl.ds(TILE + i, LANES), :] = value.astype(BF16).astype(F32)
    taps = [filt_ref[3 * g + j : 3 * g + j + 1] for j in range(3)]
    return (
        taps[0] * ext_ref[pl.ds(TILE, rows), :]
        + taps[1] * ext_ref[pl.ds(TILE - 1, rows), :]
        + taps[2] * ext_ref[pl.ds(TILE - 2, rows), :]
    )


def signal_kernel(
    a_ref, b_ref, c_ref, d_ref, filt_ref, p8_ref, r7_ref, p64_ref,
    scale_ref, sig_ref, carry_ref, send_ref, head_ref, ext_ref, u_ref, wire_ref,
):
    rows = sig_ref.shape[0]
    subs = rows // SUB
    refs = (a_ref, b_ref, c_ref, d_ref)
    tail = summed(refs, 2 * rows, EXTRA)
    for i in range(rows // LANES):
        inverse = lax.rsqrt((tail[i : i + 1] + tail[2 + i : 3 + i]) * (1.0 / D) + 1e-6)
        scale_ref[pl.ds(i * LANES, LANES), :] = jnp.broadcast_to(inverse, (LANES, LANES)).T
    streams = [stream(refs, g * rows, scale_ref, filt_ref, 1 + g, ext_ref.at[g]) for g in range(2)]
    head_ref[...] = jnp.zeros_like(head_ref)
    for g in range(2):
        head_ref[2 * g : 2 * g + 2] = streams[g][:2]
    signal = streams[0] * streams[1]
    row = lax.broadcasted_iota(jnp.int32, (rows, LANES), 0)
    sig_ref[...] = jnp.where(row < 2, 0.0, signal)
    wire_ref[HEAD:] = jnp.zeros((WIRE - HEAD, LANES), F32)
    for i, (g, at) in enumerate(((0, 0), (1, 0), (0, rows - 2), (1, rows - 2))):
        wire_ref[HEAD + 2 * i : HEAD + 2 * i + 2] = ext_ref[g, TILE + at : TILE + at + 2]
    gate = tail[4:6] * scale_ref[rows - 2 :]
    wire_ref[TAIL + 4 : TAIL + 6] = gate.astype(BF16).astype(F32)
    tiles = [[sig_ref[pl.ds(q * SUB + TILE * k, TILE), :] for k in range(STEPS)] for q in range(subs)]
    for m in range(MODES):
        real = [tiles[q][STEPS - 1] for q in range(subs)]
        imag = [None] * subs
        for k in range(STEPS - 1):
            by = [p8_ref[STEPS - 1 - k, c, m : m + 1, :] for c in range(2)]
            for q in range(subs):
                real[q] = real[q] + by[0] * tiles[q][k]
                term = by[1] * tiles[q][k]
                imag[q] = term if k == 0 else imag[q] + term
        for q in range(subs):
            turned = cmul((real[q], imag[q]), (r7_ref[m, 0], r7_ref[m, 1]))
            for c in range(2):
                u_ref[q, c, m : m + 1, :] = jnp.sum(turned[c], axis=0, keepdims=True)
    state = (jnp.zeros((MODES, LANES), F32),) * 2
    step = (p64_ref[1, 0], p64_ref[1, 1])
    for q in range(subs):
        for c in range(2):
            carry_ref[q, c] = state[c]
        state = cmul(state, step)
        state = (state[0] + u_ref[q, 0], state[1] + u_ref[q, 1])
    for c in range(2):
        wire_ref[MODES * c : MODES * (c + 1)] = state[c]
    send_ref[...] = wire_ref[...].astype(send_ref.dtype)


def edges(filt_ref, first, rim):
    def stream(g, own, old):
        taps = [filt_ref[3 * g + j : 3 * g + j + 1] for j in range(3)]
        return (
            taps[0] * own[0] + taps[1] * old[1] + taps[2] * old[0],
            taps[0] * own[1] + taps[1] * own[0] + taps[2] * old[1],
        )

    keys = stream(1, first[:2], rim[:2])
    values = stream(2, first[2:], rim[2:4])
    return keys[0] * values[0], keys[1] * values[1]


def lines(ref, at, count):
    return [ref[at + i : at + i + 1] for i in range(count)]


def impulses(plane_ref, at, pair):
    return [plane_ref[at, c] * pair[0] + plane_ref[at + 1, c] * pair[1] for c in range(2)]


def gathered(wide_ref, plane_ref, at, filt_ref, tables, alone):
    zero = jnp.zeros((MODES, LANES), F32)
    sums = [[zero, zero] for _ in tables]
    for i in range(wide_ref.shape[0]):
        value = [wide_ref[i, 0:MODES], wide_ref[i, MODES:HEAD]]
        if i or alone:
            rim = lines(wide_ref.at[i - 1], TAIL, 4) if i else [0.0] * 4
            extra = impulses(plane_ref, at, edges(filt_ref, lines(wide_ref.at[i], HEAD, 4), rim))
            value = [value[0] + extra[0], value[1] + extra[1]]
        for total, table_ref in zip(sums, tables):
            term = cmul(value, (table_ref[i, 0], table_ref[i, 1]))
            total[0], total[1] = total[0] + term[0], total[1] + term[1]
    return sums


def gate_kernel(a_ref, b_ref, c_ref, d_ref, scale_ref, filt_ref, _, gate_ref, ext_ref):
    gate_ref[...] = stream((a_ref, b_ref, c_ref, d_ref), 0, scale_ref, filt_ref, 0, ext_ref)


def plane_kernel(
    here_ref, next_ref, across_ref, before_ref, mine_tab_ref, all_tab_ref, plane_ref, filt_ref,
    mine_ref, rim_ref, send_ref, wide_ref, wire_ref,
):
    place = lax.rem(lax.axis_index("seq"), LOW)
    chip, core = lax.div(place, 2), lax.rem(place, 2)
    for i, ref in enumerate((here_ref, next_ref, across_ref, before_ref)):
        first = 2 * lax.rem(chip + i, LOW // 2)
        wide_ref[first + core] = ref[0].astype(F32)
        wide_ref[first + 1 - core] = ref[1].astype(F32)
    mine, total = gathered(wide_ref, plane_ref, 3, filt_ref, (mine_tab_ref, all_tab_ref), False)
    near = wide_ref[jnp.maximum(place - 1, 0), TAIL : TAIL + TILE]
    rim_ref[0] = jnp.where(place > 0, near, 0.0)
    rim_ref[1] = wide_ref[0, HEAD : HEAD + TILE]
    for c in range(2):
        mine_ref[c] = mine[c]
        wire_ref[c * MODES : (c + 1) * MODES] = total[c]
    wire_ref[HEAD:TAIL] = wide_ref[0, HEAD:TAIL]
    wire_ref[TAIL:] = wide_ref[LOW - 1, TAIL:]
    wire = wire_ref[...].astype(send_ref.dtype)
    for i in range(PLANES):
        send_ref[i] = wire


def final_kernel(
    got_ref, far_tab_ref, rim_ref, plane_ref, filt_ref, mine_ref, carry_ref, p64_ref, p8_ref, gt_ref, gate_ref, local_ref,
    head_ref, skip_ref, before_ref, out_ref, wide_ref, e_ref, y_ref, fix_ref,
):
    rows = gate_ref.shape[0]
    subs = rows // SUB
    for i in range(PLANES):
        wide_ref[i] = got_ref[i].astype(F32)
    (far,) = gathered(wide_ref, plane_ref, 5, filt_ref, (far_tab_ref,), True)
    far = cmul(far, (plane_ref[0, 0], plane_ref[0, 1]))
    block = lax.axis_index("seq")
    place, plane = lax.rem(block, LOW), lax.div(block, LOW)
    old = jnp.where(plane > 0, wide_ref[jnp.maximum(plane - 1, 0), TAIL : TAIL + TILE], 0.0)
    extra = impulses(plane_ref, 3, edges(filt_ref, lines(rim_ref.at[1], 0, 4), [old[i : i + 1] for i in range(4)]))
    near = cmul(extra, (plane_ref[1, 0], plane_ref[1, 1]))
    rim = rim_ref[0] + jnp.where(place > 0, 0.0, old)
    old = {1: (rim[0:1], rim[1:2]), 2: (rim[2:3], rim[3:4]), 0: (rim[4:5], rim[5:6])}
    late = {}
    for g in range(3):
        taps = [filt_ref[3 * g + j : 3 * g + j + 1] for j in range(3)]
        late[g] = (taps[1] * old[g][1] + taps[2] * old[g][0], taps[2] * old[g][1])
    pair = [
        (head_ref[i : i + 1] + late[1][i]) * (head_ref[2 + i : 3 + i] + late[2][i]) for i in range(2)
    ]
    own = impulses(plane_ref, 7, pair)
    enter = [mine_ref[c] + near[c] + far[c] + own[c] for c in range(2)]
    fix_ref[...] = jnp.zeros_like(fix_ref)
    for i in range(2):
        fix_ref[0, i : i + 1] = late[0][i]
        fix_ref[1, i : i + 1] = skip_ref[...] * pair[i]
    fix_ref[1, 0:1] -= before_ref[...] * pair[1]
    for q in range(subs):
        moved = cmul(enter, (p64_ref[q, 0], p64_ref[q, 1])) if q else enter
        for c in range(2):
            e_ref[q, c] = moved[c] + carry_ref[q, c]
    sums = [[None] * STEPS for _ in range(subs)]
    for m in range(MODES):
        table = (gt_ref[m, 0], gt_ref[m, 1])
        value = [cmul(table, (e_ref[q, 0, m : m + 1, :], e_ref[q, 1, m : m + 1, :])) for q in range(subs)]
        for k in range(STEPS):
            if k:
                by = [p8_ref[k, c, m : m + 1, :] for c in range(2)]
            for q in range(subs):
                term = by[0] * value[q][0] - by[1] * value[q][1] if k else value[q][0]
                sums[q][k] = term if m == 0 else sums[q][k] + term
    for q in range(subs):
        for k in range(STEPS):
            at = pl.ds(q * SUB + TILE * k, TILE)
            gate, conv = gate_ref[at, :], local_ref[at, :] + sums[q][k]
            if q == 0 and k == 0:
                gate, conv = gate + fix_ref[0], conv + fix_ref[1]
            y_ref[at, :] = gate * conv
    out_ref[...] = y_ref[...].T.astype(BF16)


def body(tokens, norm_gain, in_weight, short_filter, decay_reach, mode_freq, residues, skip_gain):
    rows, cols = tokens.shape
    fsdp = lax.axis_size("fsdp")
    state = shape(2, MODES, LANES)

    packed = 2 * rows + EXTRA
    weight = jnp.transpose(in_weight, (1, 0, 2))
    block = shape(packed, LANES, dtype=BF16)

    def exchange(own, *parts):
        sent = {
            d: lax.ppermute(parts[d - 1], "fsdp", [(i, (i + d) % fsdp) for i in range(fsdp)]) for d in (2, 1, 3)
        }
        return own, sent[1], sent[2], sent[3]

    products = call(
        project_kernel,
        (shape(packed, LANES), block, block, block, shape(rows, LANES), *[shape(rows, LANES, dtype=BF16)] * 3),
        (tokens, pltpu.with_memory_space_constraint(norm_gain[None], pltpu.HBM), weight),
        [
            pltpu.VMEM((rows, cols), BF16),
            pltpu.VMEM((1, cols), F32),
            pltpu.VMEM((3, cols, 4 * LANES), BF16),
            pltpu.VMEM((rows, cols), BF16),
            pltpu.VMEM((rows, LANES), F32),
            pltpu.VMEM((EXTRA, LANES), F32),
            pltpu.VMEM((rows, 4 * LANES), F32),
            pltpu.SemaphoreType.DMA((5,)),
            pltpu.SemaphoreType.DMA((3,)),
        ],
        limit=52 << 20,
        flops=2 * rows * cols * 12 * LANES,
        places=[HBM] * 3,
    )
    pair = exchange(*products[:4])
    gates = exchange(*products[4:])
    p8, r7, gt, p64, mine_tab, all_tab, far_tab, plane_tab, taps, before = call(
        table_kernel,
        (
            shape(STEPS, 2, MODES, LANES),
            shape(MODES, 2, TILE, LANES),
            shape(MODES, 2, TILE, LANES),
            shape(4, 2, MODES, LANES),
            shape(LOW, 2, MODES, LANES),
            shape(LOW, 2, MODES, LANES),
            shape(PLANES, 2, MODES, LANES),
            shape(9, 2, MODES, LANES),
            shape(SUB, LANES),
            shape(1, LANES),
        ),
        (decay_reach.T, mode_freq.T, residues.T),
        [pltpu.VMEM((2 * LOW, 2, MODES, LANES), F32)],
        flops=1 << 27,
    )
    filt = jnp.transpose(short_filter, (1, 2, 0)).reshape(9, LANES)
    skip = skip_gain[None]
    wire = shape(LOW, WIRE, LANES, dtype=BF16)
    scale, signal, carry, send, head = call(
        signal_kernel,
        (
            shape(rows, LANES), shape(rows, LANES), shape(4, 2, MODES, LANES),
            shape(WIRE, LANES, dtype=BF16), shape(TILE, LANES),
        ),
        (*pair, filt, p8, r7, p64),
        [
            pltpu.VMEM((2, TILE + rows, LANES), F32),
            pltpu.VMEM((4, 2, MODES, LANES), F32),
            pltpu.VMEM((WIRE, LANES), F32),
        ],
        flops=1 << 27,
    )
    blocks = range(LOW * PLANES)
    here = jnp.stack([send, lax.ppermute(send, "seq", [(i, i ^ 1) for i in blocks])])

    def ahead(d):
        return lax.ppermute(here, "seq", [(i, i // LOW * LOW + (i - 2 * d) % LOW) for i in blocks])

    near = [ahead(d) for d in (2, 1, 3)]
    mine, rim, send = call(
        plane_kernel,
        (state, shape(2, TILE, LANES), wire),
        (here, near[1], near[0], near[2], mine_tab, all_tab, plane_tab, filt),
        [pltpu.VMEM((LOW, WIRE, LANES), F32), pltpu.VMEM((WIRE, LANES), F32)],
        flops=1 << 24,
    )
    local_part = call(
        local_kernel,
        shape(rows, LANES),
        (signal, skip, taps, rim),
        [pltpu.VMEM((TILE + SUB, LANES), F32)],
        flops=1 << 27,
    )
    gate = call(
        gate_kernel,
        shape(rows, LANES),
        (*gates, scale, filt, local_part),
        [pltpu.VMEM((TILE + rows, LANES), F32)],
        flops=1 << 24,
    )
    line = [[LOW * j + g for j in range(PLANES)] for g in range(LOW)]
    got = lax.all_to_all(send, "seq", 0, 0, axis_index_groups=line)
    return call(
        final_kernel,
        shape(LANES, rows, dtype=BF16),
        (got, far_tab, rim, plane_tab, filt, mine, carry, p64, p8, gt, gate, local_part, head, skip, before),
        [
            pltpu.VMEM((PLANES, WIRE, LANES), F32),
            pltpu.VMEM((4, 2, MODES, LANES), F32),
            pltpu.VMEM((rows, LANES), F32),
            pltpu.VMEM((2, TILE, LANES), F32),
        ],
        flops=1 << 27,
    )


def solution(mesh):
    placed = (
        P("seq", "fsdp"),
        P("fsdp"),
        P("fsdp", None, None),
        P("fsdp", None, None),
        P("fsdp", None),
        P("fsdp", None),
        P("fsdp", None),
        P("fsdp"),
    )
    return jax.shard_map(
        body, mesh=mesh, in_specs=placed, out_specs=P("fsdp", "seq"), check_vma=False
    )
```

```python
import math

import jax
import jax.numpy as jnp
from jax import lax
from jax.experimental import pallas as pl
from jax.experimental.pallas import tpu as pltpu
from jax.sharding import PartitionSpec as P

F32 = jnp.float32
BF16 = jnp.bfloat16
D = 8192
MODES = 16
LANES = 128
TILE = 8
SUB = 64
STEPS = SUB // TILE
LOW = 8
PLANES = 8
HEAD = 2 * MODES
TAIL = HEAD + 4
EXTRA = 16
WIRE = 48
VMEM = pl.BlockSpec(memory_space=pltpu.VMEM)
HBM = pl.BlockSpec(memory_space=pltpu.HBM)


def call(kernel, out_shape, operands, scratch=(), limit=16 << 20, flops=0, places=None):
    moved = sum(math.prod(v.shape) * v.dtype.itemsize for v in (*operands, *jax.tree.leaves(out_shape)))
    return pl.pallas_call(
        kernel,
        out_shape=out_shape,
        in_specs=places or [VMEM] * len(operands),
        out_specs=jax.tree.map(lambda _: VMEM, out_shape),
        scratch_shapes=list(scratch),
        compiler_params=pltpu.CompilerParams(vmem_limit_bytes=limit),
        cost_estimate=pl.CostEstimate(flops=flops, bytes_accessed=moved, transcendentals=0),
    )(*operands)


def shape(*dims, dtype=F32):
    return jax.ShapeDtypeStruct(dims, dtype)


def cmul(a, b):
    return a[0] * b[0] - a[1] * b[1], a[0] * b[1] + a[1] * b[0]


def turn(angle):
    cycles = jnp.floor(angle * (0.5 / math.pi) + 0.5)
    rest = angle - cycles * 6.28125
    rest = rest - cycles * 1.93500518798828125e-3
    rest = rest - cycles * 3.0199159819e-7
    return jnp.cos(rest), jnp.sin(rest)


def table_kernel(
    reach_ref, freq_ref, res_ref, p8_ref, r7_ref, gt_ref, p64_ref, mine_ref, all_ref, far_ref, plane_ref, h_ref, before_ref, power_ref
):
    rate = 1.0 / reach_ref[...]
    freq = freq_ref[...]
    gain = res_ref[...] * jnp.sqrt(2.0 * rate)
    block = lax.axis_index("seq")
    place = lax.rem(block, LOW)
    plane = lax.div(block, LOW)

    def power(n):
        size = jnp.exp(-rate * n)
        cosine, sine = turn(freq * n)
        return size * cosine, size * sine

    one = (jnp.ones_like(rate), jnp.zeros_like(rate))

    def chain(base, count):
        values = [one]
        for _ in range(count - 1):
            values.append(cmul(values[-1], base))
        return values

    ones = chain(power(1.0), TILE + 1)
    for j in range(TILE):
        for c in range(2):
            r7_ref[:, c, j, :] = ones[TILE - 1 - j][c]
            gt_ref[:, c, j, :] = gain * ones[j + 1][c]
    eights = chain(power(8.0), STEPS)
    for k in range(STEPS):
        for c in range(2):
            p8_ref[k, c] = eights[k][c]
    for q, value in enumerate(chain(power(float(SUB)), 4)):
        for c in range(2):
            p64_ref[q, c] = value[c]
    blocks = chain(power(256.0), LOW)
    for k, value in enumerate(blocks):
        for c in range(2):
            power_ref[k, c] = jnp.zeros_like(rate)
            power_ref[LOW + k, c] = value[c]
    for i in range(LOW):
        for c in range(2):
            mine_ref[i, c] = power_ref[LOW - 1 - i + place, c]
            all_ref[i, c] = blocks[LOW - 1 - i][c]
    unit, far = power(1.0), power(2048.0)
    size = jnp.exp(2.0 * rate)
    back = (size * unit[0], -size * unit[1])
    twice = cmul(back, back)
    last = cmul(blocks[1], back)
    earlier = cmul(last, back)
    rows = (
        (power_ref[LOW + place, 0], power_ref[LOW + place, 1]),
        (power_ref[LOW - 1 + place, 0], power_ref[LOW - 1 + place, 1]),
        far,
        last,
        earlier,
        cmul(last, blocks[LOW - 1]),
        cmul(earlier, blocks[LOW - 1]),
        back,
        twice,
    )
    for i, value in enumerate(rows):
        for c in range(2):
            plane_ref[i, c] = value[c]
    for k, value in enumerate(chain(far, PLANES)):
        for c in range(2):
            power_ref[LOW + k, c] = value[c]
    for i in range(PLANES):
        for c in range(2):
            far_ref[i, c] = power_ref[LOW - 1 - i + plane, c]
    before_ref[...] = jnp.sum(gain * back[0], axis=0, keepdims=True)
    taps = [jnp.zeros((TILE, LANES), F32) for _ in range(STEPS)]
    row = lax.broadcasted_iota(jnp.int32, (TILE, LANES), 0)
    for m in range(MODES):
        real = jnp.where(row == 0, gain[m : m + 1], pltpu.roll(gt_ref[m, 0], 1, 0))
        imag = jnp.where(row == 0, 0.0, pltpu.roll(gt_ref[m, 1], 1, 0))
        for k in range(STEPS):
            taps[k] = taps[k] + (eights[k][0][m : m + 1] * real - eights[k][1][m : m + 1] * imag)
    for k in range(STEPS):
        h_ref[TILE * k : TILE * k + TILE] = taps[k]


def project_kernel(
    tok_hbm, gain_hbm, w_hbm, own_ref, one_ref, two_ref, three_ref, own_gate, one_gate, two_gate, three_gate,
    tok_ref, gain_ref, w_ref, xg_ref, acc_ref, ext_ref, got_ref, sems, w_sems,
):
    rows, cols = tok_ref.shape
    outs = (own_ref, one_ref, two_ref, three_ref)
    gates = (own_gate, one_gate, two_gate, three_gate)
    pieces = 4
    span = rows // pieces
    gain_copy = pltpu.make_async_copy(gain_hbm, gain_ref, sems.at[0])
    gain_copy.start()
    tok_copies = []
    for i in range(pieces):
        at = pl.ds(i * span, span)
        tok_copies.append(pltpu.make_async_copy(tok_hbm.at[at], tok_ref.at[at], sems.at[1 + i]))
        tok_copies[-1].start(priority=i % 2)
    w_copies = [pltpu.make_async_copy(w_hbm.at[(g + 1) % 3], w_ref.at[g], w_sems.at[g]) for g in range(3)]
    w_copies[0].start(priority=0)
    w_copies[1].start(priority=1)
    gain_copy.wait()
    gain = gain_ref[...]
    for i in range(pieces):
        tok_copies[i].wait()
        if i == 1:
            w_copies[2].start(priority=0)
        for lo in range(i * span, (i + 1) * span, 32):
            x = tok_ref[pl.ds(lo, 32), :].astype(F32)
            xg_ref[pl.ds(lo, 32), :] = (x * gain).astype(BF16)
    me = lax.axis_index("fsdp")
    for g in range(3):
        w_copies[g].wait()
        got_ref[...] = jnp.dot(xg_ref[...], w_ref[g], preferred_element_type=F32).astype(BF16)
        if g == 0:
            for lo in range(0, rows, 32):
                x = tok_ref[pl.ds(lo, 32), :].astype(F32)
                sq = x * x
                acc_ref[pl.ds(lo, 32), :] = sum(sq[:, j : j + LANES] for j in range(0, cols, LANES))
        for d in range(4):
            at = pl.ds(pl.multiple_of(lax.rem(me + d, 4) * LANES, LANES), LANES)
            if g < 2:
                outs[d][g * rows : (g + 1) * rows] = got_ref[:, at]
            else:
                gates[d][...] = got_ref[:, at]
    acc = acc_ref[...]
    high = acc.astype(BF16)
    mid = (acc - high.astype(F32)).astype(BF16)
    ones = jnp.ones((16, LANES), BF16)
    dims = (((1,), (1,)), ((), ()))
    total = (
        lax.dot_general(ones, high, dims, preferred_element_type=F32)
        + lax.dot_general(ones, mid, dims, preferred_element_type=F32)
    )[:1]
    ext_ref[...] = jnp.zeros_like(ext_ref)
    for i in range(rows // LANES):
        value = total[:, i * LANES : (i + 1) * LANES]
        high = value.astype(BF16).astype(F32)
        ext_ref[i : i + 1] = high
        ext_ref[2 + i : 3 + i] = value - high
    for d in range(4):
        at = pl.ds(pl.multiple_of(lax.rem(me + d, 4) * LANES, LANES), LANES)
        ext_ref[4:6] = got_ref[rows - EXTRA :, at].astype(F32)[EXTRA - 2 :]
        outs[d][2 * rows :] = ext_ref[...].astype(outs[d].dtype)


def local_kernel(sig_ref, skip_ref, h_ref, _, out_ref, pad_ref):
    pad_ref[0:TILE] = jnp.zeros((TILE, LANES), F32)
    for q in range(sig_ref.shape[0] // SUB):
        pad_ref[TILE:] = sig_ref[pl.ds(q * SUB, SUB), :]
        sums = [skip_ref[...] * pad_ref[pl.ds(TILE + TILE * i, TILE), :] for i in range(STEPS)]
        for b in range(TILE):
            moved = [pad_ref[pl.ds(TILE + TILE * i - b, TILE), :] for i in range(STEPS)]
            for a in range(STEPS):
                tap = h_ref[TILE * a + b : TILE * a + b + 1, :]
                for i in range(a, STEPS):
                    sums[i] = sums[i] + tap * moved[i - a]
        for i in range(STEPS):
            out_ref[pl.ds(q * SUB + TILE * i, TILE), :] = sums[i]


def summed(refs, lo, n):
    at = pl.ds(lo, n)
    return refs[0][at, :].astype(F32) + (refs[1][at, :].astype(F32) + refs[2][at, :].astype(F32) + refs[3][at, :].astype(F32))


def stream(refs, lo, scale_ref, filt_ref, g, ext_ref):
    rows = scale_ref.shape[0]
    ext_ref[0:TILE] = jnp.zeros((TILE, LANES), F32)
    for i in range(0, rows, LANES):
        value = summed(refs, lo + i, LANES) * scale_ref[pl.ds(i, LANES), :]
        ext_ref[pl.ds(TILE + i, LANES), :] = value.astype(BF16).astype(F32)
    taps = [filt_ref[3 * g + j : 3 * g + j + 1] for j in range(3)]
    return (
        taps[0] * ext_ref[pl.ds(TILE, rows), :]
        + taps[1] * ext_ref[pl.ds(TILE - 1, rows), :]
        + taps[2] * ext_ref[pl.ds(TILE - 2, rows), :]
    )


def signal_kernel(
    a_ref, b_ref, c_ref, d_ref, filt_ref, p8_ref, r7_ref, p64_ref,
    scale_ref, sig_ref, carry_ref, send_ref, head_ref, ext_ref, u_ref, wire_ref,
):
    rows = sig_ref.shape[0]
    subs = rows // SUB
    refs = (a_ref, b_ref, c_ref, d_ref)
    tail = summed(refs, 2 * rows, EXTRA)
    for i in range(rows // LANES):
        inverse = lax.rsqrt((tail[i : i + 1] + tail[2 + i : 3 + i]) * (1.0 / D) + 1e-6)
        scale_ref[pl.ds(i * LANES, LANES), :] = jnp.broadcast_to(inverse, (LANES, LANES)).T
    streams = [stream(refs, g * rows, scale_ref, filt_ref, 1 + g, ext_ref.at[g]) for g in range(2)]
    head_ref[...] = jnp.zeros_like(head_ref)
    for g in range(2):
        head_ref[2 * g : 2 * g + 2] = streams[g][:2]
    signal = streams[0] * streams[1]
    row = lax.broadcasted_iota(jnp.int32, (rows, LANES), 0)
    sig_ref[...] = jnp.where(row < 2, 0.0, signal)
    wire_ref[HEAD:] = jnp.zeros((WIRE - HEAD, LANES), F32)
    for i, (g, at) in enumerate(((0, 0), (1, 0), (0, rows - 2), (1, rows - 2))):
        wire_ref[HEAD + 2 * i : HEAD + 2 * i + 2] = ext_ref[g, TILE + at : TILE + at + 2]
    gate = tail[4:6] * scale_ref[rows - 2 :]
    wire_ref[TAIL + 4 : TAIL + 6] = gate.astype(BF16).astype(F32)
    tiles = [[sig_ref[pl.ds(q * SUB + TILE * k, TILE), :] for k in range(STEPS)] for q in range(subs)]
    for m in range(MODES):
        real = [tiles[q][STEPS - 1] for q in range(subs)]
        imag = [None] * subs
        for k in range(STEPS - 1):
            by = [p8_ref[STEPS - 1 - k, c, m : m + 1, :] for c in range(2)]
            for q in range(subs):
                real[q] = real[q] + by[0] * tiles[q][k]
                term = by[1] * tiles[q][k]
                imag[q] = term if k == 0 else imag[q] + term
        for q in range(subs):
            turned = cmul((real[q], imag[q]), (r7_ref[m, 0], r7_ref[m, 1]))
            for c in range(2):
                u_ref[q, c, m : m + 1, :] = jnp.sum(turned[c], axis=0, keepdims=True)
    state = (jnp.zeros((MODES, LANES), F32),) * 2
    step = (p64_ref[1, 0], p64_ref[1, 1])
    for q in range(subs):
        for c in range(2):
            carry_ref[q, c] = state[c]
        state = cmul(state, step)
        state = (state[0] + u_ref[q, 0], state[1] + u_ref[q, 1])
    for c in range(2):
        wire_ref[MODES * c : MODES * (c + 1)] = state[c]
    send_ref[...] = wire_ref[...].astype(send_ref.dtype)


def edges(filt_ref, first, rim):
    def stream(g, own, old):
        taps = [filt_ref[3 * g + j : 3 * g + j + 1] for j in range(3)]
        return (
            taps[0] * own[0] + taps[1] * old[1] + taps[2] * old[0],
            taps[0] * own[1] + taps[1] * own[0] + taps[2] * old[1],
        )

    keys = stream(1, first[:2], rim[:2])
    values = stream(2, first[2:], rim[2:4])
    return keys[0] * values[0], keys[1] * values[1]


def lines(ref, at, count):
    return [ref[at + i : at + i + 1] for i in range(count)]


def impulses(plane_ref, at, pair):
    return [plane_ref[at, c] * pair[0] + plane_ref[at + 1, c] * pair[1] for c in range(2)]


def gathered(wide_ref, plane_ref, at, filt_ref, tables, alone):
    zero = jnp.zeros((MODES, LANES), F32)
    sums = [[zero, zero] for _ in tables]
    for i in range(wide_ref.shape[0]):
        value = [wide_ref[i, 0:MODES], wide_ref[i, MODES:HEAD]]
        if i or alone:
            rim = lines(wide_ref.at[i - 1], TAIL, 4) if i else [0.0] * 4
            extra = impulses(plane_ref, at, edges(filt_ref, lines(wide_ref.at[i], HEAD, 4), rim))
            value = [value[0] + extra[0], value[1] + extra[1]]
        for total, table_ref in zip(sums, tables):
            term = cmul(value, (table_ref[i, 0], table_ref[i, 1]))
            total[0], total[1] = total[0] + term[0], total[1] + term[1]
    return sums


def gate_kernel(a_ref, b_ref, c_ref, d_ref, scale_ref, filt_ref, _, gate_ref, ext_ref):
    gate_ref[...] = stream((a_ref, b_ref, c_ref, d_ref), 0, scale_ref, filt_ref, 0, ext_ref)


def plane_kernel(
    here_ref, next_ref, across_ref, before_ref, mine_tab_ref, all_tab_ref, plane_ref, filt_ref,
    mine_ref, rim_ref, send_ref, wide_ref, wire_ref,
):
    place = lax.rem(lax.axis_index("seq"), LOW)
    chip, core = lax.div(place, 2), lax.rem(place, 2)
    for i, ref in enumerate((here_ref, next_ref, across_ref, before_ref)):
        first = 2 * lax.rem(chip + i, LOW // 2)
        wide_ref[first + core] = ref[0].astype(F32)
        wide_ref[first + 1 - core] = ref[1].astype(F32)
    mine, total = gathered(wide_ref, plane_ref, 3, filt_ref, (mine_tab_ref, all_tab_ref), False)
    near = wide_ref[jnp.maximum(place - 1, 0), TAIL : TAIL + TILE]
    rim_ref[0] = jnp.where(place > 0, near, 0.0)
    rim_ref[1] = wide_ref[0, HEAD : HEAD + TILE]
    for c in range(2):
        mine_ref[c] = mine[c]
        wire_ref[c * MODES : (c + 1) * MODES] = total[c]
    wire_ref[HEAD:TAIL] = wide_ref[0, HEAD:TAIL]
    wire_ref[TAIL:] = wide_ref[LOW - 1, TAIL:]
    wire = wire_ref[...].astype(send_ref.dtype)
    for i in range(PLANES):
        send_ref[i] = wire


def final_kernel(
    got_ref, far_tab_ref, rim_ref, plane_ref, filt_ref, mine_ref, carry_ref, p64_ref, p8_ref, gt_ref, gate_ref, local_ref,
    head_ref, skip_ref, before_ref, out_ref, wide_ref, e_ref, y_ref, fix_ref,
):
    rows = gate_ref.shape[0]
    subs = rows // SUB
    for i in range(PLANES):
        wide_ref[i] = got_ref[i].astype(F32)
    (far,) = gathered(wide_ref, plane_ref, 5, filt_ref, (far_tab_ref,), True)
    far = cmul(far, (plane_ref[0, 0], plane_ref[0, 1]))
    block = lax.axis_index("seq")
    place, plane = lax.rem(block, LOW), lax.div(block, LOW)
    old = jnp.where(plane > 0, wide_ref[jnp.maximum(plane - 1, 0), TAIL : TAIL + TILE], 0.0)
    extra = impulses(plane_ref, 3, edges(filt_ref, lines(rim_ref.at[1], 0, 4), [old[i : i + 1] for i in range(4)]))
    near = cmul(extra, (plane_ref[1, 0], plane_ref[1, 1]))
    rim = rim_ref[0] + jnp.where(place > 0, 0.0, old)
    old = {1: (rim[0:1], rim[1:2]), 2: (rim[2:3], rim[3:4]), 0: (rim[4:5], rim[5:6])}
    late = {}
    for g in range(3):
        taps = [filt_ref[3 * g + j : 3 * g + j + 1] for j in range(3)]
        late[g] = (taps[1] * old[g][1] + taps[2] * old[g][0], taps[2] * old[g][1])
    pair = [
        (head_ref[i : i + 1] + late[1][i]) * (head_ref[2 + i : 3 + i] + late[2][i]) for i in range(2)
    ]
    own = impulses(plane_ref, 7, pair)
    enter = [mine_ref[c] + near[c] + far[c] + own[c] for c in range(2)]
    fix_ref[...] = jnp.zeros_like(fix_ref)
    for i in range(2):
        fix_ref[0, i : i + 1] = late[0][i]
        fix_ref[1, i : i + 1] = skip_ref[...] * pair[i]
    fix_ref[1, 0:1] -= before_ref[...] * pair[1]
    for q in range(subs):
        moved = cmul(enter, (p64_ref[q, 0], p64_ref[q, 1])) if q else enter
        for c in range(2):
            e_ref[q, c] = moved[c] + carry_ref[q, c]
    sums = [[None] * STEPS for _ in range(subs)]
    for m in range(MODES):
        table = (gt_ref[m, 0], gt_ref[m, 1])
        value = [cmul(table, (e_ref[q, 0, m : m + 1, :], e_ref[q, 1, m : m + 1, :])) for q in range(subs)]
        for k in range(STEPS):
            if k:
                by = [p8_ref[k, c, m : m + 1, :] for c in range(2)]
            for q in range(subs):
                term = by[0] * value[q][0] - by[1] * value[q][1] if k else value[q][0]
                sums[q][k] = term if m == 0 else sums[q][k] + term
    for q in range(subs):
        for k in range(STEPS):
            at = pl.ds(q * SUB + TILE * k, TILE)
            gate, conv = gate_ref[at, :], local_ref[at, :] + sums[q][k]
            if q == 0 and k == 0:
                gate, conv = gate + fix_ref[0], conv + fix_ref[1]
            y_ref[at, :] = gate * conv
    out_ref[...] = y_ref[...].T.astype(BF16)


def body(tokens, norm_gain, in_weight, short_filter, decay_reach, mode_freq, residues, skip_gain):
    rows, cols = tokens.shape
    fsdp = lax.axis_size("fsdp")
    state = shape(2, MODES, LANES)

    packed = 2 * rows + EXTRA
    weight = jnp.transpose(in_weight, (1, 0, 2))
    block = shape(packed, LANES, dtype=BF16)

    def exchange(own, *parts):
        sent = {
            d: lax.ppermute(parts[d - 1], "fsdp", [(i, (i + d) % fsdp) for i in range(fsdp)]) for d in (2, 1, 3)
        }
        return own, sent[1], sent[2], sent[3]

    products = call(
        project_kernel,
        ([block] * 4 + [shape(rows, LANES, dtype=BF16)] * 4),
        (tokens, pltpu.with_memory_space_constraint(norm_gain[None], pltpu.HBM), weight),
        [
            pltpu.VMEM((rows, cols), BF16),
            pltpu.VMEM((1, cols), F32),
            pltpu.VMEM((3, cols, 4 * LANES), BF16),
            pltpu.VMEM((rows, cols), BF16),
            pltpu.VMEM((rows, LANES), F32),
            pltpu.VMEM((EXTRA, LANES), F32),
            pltpu.VMEM((rows, 4 * LANES), BF16),
            pltpu.SemaphoreType.DMA((5,)),
            pltpu.SemaphoreType.DMA((3,)),
        ],
        limit=52 << 20,
        flops=2 * rows * cols * 12 * LANES,
        places=[HBM] * 3,
    )
    pair = exchange(*products[:4])
    gates = exchange(*products[4:])
    p8, r7, gt, p64, mine_tab, all_tab, far_tab, plane_tab, taps, before = call(
        table_kernel,
        (
            shape(STEPS, 2, MODES, LANES),
            shape(MODES, 2, TILE, LANES),
            shape(MODES, 2, TILE, LANES),
            shape(4, 2, MODES, LANES),
            shape(LOW, 2, MODES, LANES),
            shape(LOW, 2, MODES, LANES),
            shape(PLANES, 2, MODES, LANES),
            shape(9, 2, MODES, LANES),
            shape(SUB, LANES),
            shape(1, LANES),
        ),
        (decay_reach.T, mode_freq.T, residues.T),
        [pltpu.VMEM((2 * LOW, 2, MODES, LANES), F32)],
        flops=1 << 27,
    )
    filt = jnp.transpose(short_filter, (1, 2, 0)).reshape(9, LANES)
    skip = skip_gain[None]
    wire = shape(LOW, WIRE, LANES, dtype=BF16)
    scale, signal, carry, send, head = call(
        signal_kernel,
        (
            shape(rows, LANES), shape(rows, LANES), shape(4, 2, MODES, LANES),
            shape(WIRE, LANES, dtype=BF16), shape(TILE, LANES),
        ),
        (*pair, filt, p8, r7, p64),
        [
            pltpu.VMEM((2, TILE + rows, LANES), F32),
            pltpu.VMEM((4, 2, MODES, LANES), F32),
            pltpu.VMEM((WIRE, LANES), F32),
        ],
        flops=1 << 27,
    )
    blocks = range(LOW * PLANES)
    here = jnp.stack([send, lax.ppermute(send, "seq", [(i, i ^ 1) for i in blocks])])

    def ahead(d):
        return lax.ppermute(here, "seq", [(i, i // LOW * LOW + (i - 2 * d) % LOW) for i in blocks])

    near = [ahead(d) for d in (2, 1, 3)]
    mine, rim, send = call(
        plane_kernel,
        (state, shape(2, TILE, LANES), wire),
        (here, near[1], near[0], near[2], mine_tab, all_tab, plane_tab, filt),
        [pltpu.VMEM((LOW, WIRE, LANES), F32), pltpu.VMEM((WIRE, LANES), F32)],
        flops=1 << 24,
    )
    local_part = call(
        local_kernel,
        shape(rows, LANES),
        (signal, skip, taps, rim),
        [pltpu.VMEM((TILE + SUB, LANES), F32)],
        flops=1 << 27,
    )
    gate = call(
        gate_kernel,
        shape(rows, LANES),
        (*gates, scale, filt, local_part),
        [pltpu.VMEM((TILE + rows, LANES), F32)],
        flops=1 << 24,
    )
    line = [[LOW * j + g for j in range(PLANES)] for g in range(LOW)]
    got = lax.all_to_all(send, "seq", 0, 0, axis_index_groups=line)
    return call(
        final_kernel,
        shape(LANES, rows, dtype=BF16),
        (got, far_tab, rim, plane_tab, filt, mine, carry, p64, p8, gt, gate, local_part, head, skip, before),
        [
            pltpu.VMEM((PLANES, WIRE, LANES), F32),
            pltpu.VMEM((4, 2, MODES, LANES), F32),
            pltpu.VMEM((rows, LANES), F32),
            pltpu.VMEM((2, TILE, LANES), F32),
        ],
        flops=1 << 27,
    )


def solution(mesh):
    placed = (
        P("seq", "fsdp"),
        P("fsdp"),
        P("fsdp", None, None),
        P("fsdp", None, None),
        P("fsdp", None),
        P("fsdp", None),
        P("fsdp", None),
        P("fsdp"),
    )
    return jax.shard_map(
        body, mesh=mesh, in_specs=placed, out_specs=P("fsdp", "seq"), check_vma=False
    )
```

```python
import math

import jax
import jax.numpy as jnp
from jax import lax
from jax.experimental import pallas as pl
from jax.experimental.pallas import tpu as pltpu
from jax.sharding import PartitionSpec as P

F32 = jnp.float32
BF16 = jnp.bfloat16
D = 8192
MODES = 16
LANES = 128
TILE = 8
SUB = 64
STEPS = SUB // TILE
LOW = 8
PLANES = 8
HEAD = 2 * MODES
TAIL = HEAD + 4
EXTRA = 16
WIRE = 48
VMEM = pl.BlockSpec(memory_space=pltpu.VMEM)
HBM = pl.BlockSpec(memory_space=pltpu.HBM)


def call(kernel, out_shape, operands, scratch=(), limit=16 << 20, flops=0, places=None):
    moved = sum(math.prod(v.shape) * v.dtype.itemsize for v in (*operands, *jax.tree.leaves(out_shape)))
    return pl.pallas_call(
        kernel,
        out_shape=out_shape,
        in_specs=places or [VMEM] * len(operands),
        out_specs=jax.tree.map(lambda _: VMEM, out_shape),
        scratch_shapes=list(scratch),
        compiler_params=pltpu.CompilerParams(vmem_limit_bytes=limit),
        cost_estimate=pl.CostEstimate(flops=flops, bytes_accessed=moved, transcendentals=0),
    )(*operands)


def shape(*dims, dtype=F32):
    return jax.ShapeDtypeStruct(dims, dtype)


def cmul(a, b):
    return a[0] * b[0] - a[1] * b[1], a[0] * b[1] + a[1] * b[0]


def turn(angle):
    cycles = jnp.floor(angle * (0.5 / math.pi) + 0.5)
    rest = angle - cycles * 6.28125
    rest = rest - cycles * 1.93500518798828125e-3
    rest = rest - cycles * 3.0199159819e-7
    return jnp.cos(rest), jnp.sin(rest)


def table_kernel(
    reach_ref, freq_ref, res_ref, p8_ref, r7_ref, gt_ref, p64_ref, mine_ref, all_ref, far_ref, plane_ref, h_ref, before_ref, power_ref
):
    rate = 1.0 / reach_ref[...]
    freq = freq_ref[...]
    gain = res_ref[...] * jnp.sqrt(2.0 * rate)
    block = lax.axis_index("seq")
    place = lax.rem(block, LOW)
    plane = lax.div(block, LOW)

    def power(n):
        size = jnp.exp(-rate * n)
        cosine, sine = turn(freq * n)
        return size * cosine, size * sine

    one = (jnp.ones_like(rate), jnp.zeros_like(rate))

    def chain(base, count):
        values = [one]
        for _ in range(count - 1):
            values.append(cmul(values[-1], base))
        return values

    ones = chain(power(1.0), TILE + 1)
    for j in range(TILE):
        for c in range(2):
            r7_ref[:, c, j, :] = ones[TILE - 1 - j][c]
            gt_ref[:, c, j, :] = gain * ones[j + 1][c]
    eights = chain(power(8.0), STEPS)
    for k in range(STEPS):
        for c in range(2):
            p8_ref[k, c] = eights[k][c]
    for q, value in enumerate(chain(power(float(SUB)), 4)):
        for c in range(2):
            p64_ref[q, c] = value[c]
    blocks = chain(power(256.0), LOW)
    for k, value in enumerate(blocks):
        for c in range(2):
            power_ref[k, c] = jnp.zeros_like(rate)
            power_ref[LOW + k, c] = value[c]
    for i in range(LOW):
        for c in range(2):
            mine_ref[i, c] = power_ref[LOW - 1 - i + place, c]
            all_ref[i, c] = blocks[LOW - 1 - i][c]
    unit, far = power(1.0), power(2048.0)
    size = jnp.exp(2.0 * rate)
    back = (size * unit[0], -size * unit[1])
    twice = cmul(back, back)
    last = cmul(blocks[1], back)
    earlier = cmul(last, back)
    rows = (
        (power_ref[LOW + place, 0], power_ref[LOW + place, 1]),
        (power_ref[LOW - 1 + place, 0], power_ref[LOW - 1 + place, 1]),
        far,
        last,
        earlier,
        cmul(last, blocks[LOW - 1]),
        cmul(earlier, blocks[LOW - 1]),
        back,
        twice,
    )
    for i, value in enumerate(rows):
        for c in range(2):
            plane_ref[i, c] = value[c]
    for k, value in enumerate(chain(far, PLANES)):
        for c in range(2):
            power_ref[LOW + k, c] = value[c]
    for i in range(PLANES):
        for c in range(2):
            far_ref[i, c] = power_ref[LOW - 1 - i + plane, c]
    before_ref[...] = jnp.sum(gain * back[0], axis=0, keepdims=True)
    taps = [jnp.zeros((TILE, LANES), F32) for _ in range(STEPS)]
    row = lax.broadcasted_iota(jnp.int32, (TILE, LANES), 0)
    for m in range(MODES):
        real = jnp.where(row == 0, gain[m : m + 1], pltpu.roll(gt_ref[m, 0], 1, 0))
        imag = jnp.where(row == 0, 0.0, pltpu.roll(gt_ref[m, 1], 1, 0))
        for k in range(STEPS):
            taps[k] = taps[k] + (eights[k][0][m : m + 1] * real - eights[k][1][m : m + 1] * imag)
    for k in range(STEPS):
        h_ref[TILE * k : TILE * k + TILE] = taps[k]


def project_kernel(
    tok_hbm, gain_hbm, w_hbm, own_ref, one_ref, two_ref, three_ref, own_gate, one_gate, two_gate, three_gate,
    tok_ref, gain_ref, w_ref, xg_ref, acc_ref, ext_ref, got_ref, sems, w_sems,
):
    rows, cols = tok_ref.shape
    outs = (own_ref, one_ref, two_ref, three_ref)
    gates = (own_gate, one_gate, two_gate, three_gate)
    pieces = 8
    span = rows // pieces
    gain_copy = pltpu.make_async_copy(gain_hbm, gain_ref, sems.at[0])
    gain_copy.start()
    tok_copies = []
    for i in range(pieces):
        at = pl.ds(i * span, span)
        tok_copies.append(pltpu.make_async_copy(tok_hbm.at[at], tok_ref.at[at], sems.at[1 + i]))
        tok_copies[-1].start(priority=i % 2)
    w_copies = [pltpu.make_async_copy(w_hbm.at[(g + 1) % 3], w_ref.at[g], w_sems.at[g]) for g in range(3)]
    w_copies[0].start(priority=0)
    w_copies[1].start(priority=1)
    gain_copy.wait()
    gain = gain_ref[...]
    for i in range(pieces):
        tok_copies[i].wait()
        if i == 3:
            w_copies[2].start(priority=0)
        for lo in range(i * span, (i + 1) * span, 32):
            x = tok_ref[pl.ds(lo, 32), :].astype(F32)
            xg_ref[pl.ds(lo, 32), :] = (x * gain).astype(BF16)
    me = lax.axis_index("fsdp")
    for g in range(3):
        w_copies[g].wait()
        got_ref[...] = jnp.dot(xg_ref[...], w_ref[g], preferred_element_type=F32)
        if g == 0:
            for lo in range(0, rows, 32):
                x = tok_ref[pl.ds(lo, 32), :].astype(F32)
                sq = x * x
                acc_ref[pl.ds(lo, 32), :] = sum(sq[:, j : j + LANES] for j in range(0, cols, LANES))
        for d in range(4):
            at = pl.ds(pl.multiple_of(lax.rem(me + d, 4) * LANES, LANES), LANES)
            if g < 2:
                outs[d][g * rows : (g + 1) * rows] = got_ref[:, at].astype(outs[d].dtype)
            else:
                gates[d][...] = got_ref[:, at].astype(gates[d].dtype)
    acc = acc_ref[...]
    high = acc.astype(BF16)
    mid = (acc - high.astype(F32)).astype(BF16)
    ones = jnp.ones((16, LANES), BF16)
    dims = (((1,), (1,)), ((), ()))
    total = (
        lax.dot_general(ones, high, dims, preferred_element_type=F32)
        + lax.dot_general(ones, mid, dims, preferred_element_type=F32)
    )[:1]
    ext_ref[...] = jnp.zeros_like(ext_ref)
    for i in range(rows // LANES):
        value = total[:, i * LANES : (i + 1) * LANES]
        high = value.astype(BF16).astype(F32)
        ext_ref[i : i + 1] = high
        ext_ref[2 + i : 3 + i] = value - high
    for d in range(4):
        at = pl.ds(pl.multiple_of(lax.rem(me + d, 4) * LANES, LANES), LANES)
        ext_ref[4:6] = got_ref[rows - 2 : rows, at]
        outs[d][2 * rows :] = ext_ref[...].astype(outs[d].dtype)


def local_kernel(sig_ref, skip_ref, h_ref, _, out_ref, pad_ref):
    pad_ref[0:TILE] = jnp.zeros((TILE, LANES), F32)
    for q in range(sig_ref.shape[0] // SUB):
        pad_ref[TILE:] = sig_ref[pl.ds(q * SUB, SUB), :]
        sums = [skip_ref[...] * pad_ref[pl.ds(TILE + TILE * i, TILE), :] for i in range(STEPS)]
        for b in range(TILE):
            moved = [pad_ref[pl.ds(TILE + TILE * i - b, TILE), :] for i in range(STEPS)]
            for a in range(STEPS):
                tap = h_ref[TILE * a + b : TILE * a + b + 1, :]
                for i in range(a, STEPS):
                    sums[i] = sums[i] + tap * moved[i - a]
        for i in range(STEPS):
            out_ref[pl.ds(q * SUB + TILE * i, TILE), :] = sums[i]


def summed(refs, lo, n):
    at = pl.ds(lo, n)
    return refs[0][at, :] + (refs[1][at, :].astype(F32) + refs[2][at, :].astype(F32) + refs[3][at, :].astype(F32))


def stream(refs, lo, scale_ref, filt_ref, g, ext_ref):
    rows = scale_ref.shape[0]
    ext_ref[0:TILE] = jnp.zeros((TILE, LANES), F32)
    for i in range(0, rows, LANES):
        value = summed(refs, lo + i, LANES) * scale_ref[pl.ds(i, LANES), :]
        ext_ref[pl.ds(TILE + i, LANES), :] = value.astype(BF16).astype(F32)
    taps = [filt_ref[3 * g + j : 3 * g + j + 1] for j in range(3)]
    return (
        taps[0] * ext_ref[pl.ds(TILE, rows), :]
        + taps[1] * ext_ref[pl.ds(TILE - 1, rows), :]
        + taps[2] * ext_ref[pl.ds(TILE - 2, rows), :]
    )


def signal_kernel(
    a_ref, b_ref, c_ref, d_ref, filt_ref, p8_ref, r7_ref, p64_ref,
    scale_ref, sig_ref, carry_ref, send_ref, head_ref, ext_ref, u_ref, wire_ref,
):
    rows = sig_ref.shape[0]
    subs = rows // SUB
    refs = (a_ref, b_ref, c_ref, d_ref)
    tail = summed(refs, 2 * rows, EXTRA)
    for i in range(rows // LANES):
        inverse = lax.rsqrt((tail[i : i + 1] + tail[2 + i : 3 + i]) * (1.0 / D) + 1e-6)
        scale_ref[pl.ds(i * LANES, LANES), :] = jnp.broadcast_to(inverse, (LANES, LANES)).T
    streams = [stream(refs, g * rows, scale_ref, filt_ref, 1 + g, ext_ref.at[g]) for g in range(2)]
    head_ref[...] = jnp.zeros_like(head_ref)
    for g in range(2):
        head_ref[2 * g : 2 * g + 2] = streams[g][:2]
    signal = streams[0] * streams[1]
    row = lax.broadcasted_iota(jnp.int32, (rows, LANES), 0)
    sig_ref[...] = jnp.where(row < 2, 0.0, signal)
    wire_ref[HEAD:] = jnp.zeros((WIRE - HEAD, LANES), F32)
    for i, (g, at) in enumerate(((0, 0), (1, 0), (0, rows - 2), (1, rows - 2))):
        wire_ref[HEAD + 2 * i : HEAD + 2 * i + 2] = ext_ref[g, TILE + at : TILE + at + 2]
    gate = tail[4:6] * scale_ref[rows - 2 :]
    wire_ref[TAIL + 4 : TAIL + 6] = gate.astype(BF16).astype(F32)
    tiles = [[sig_ref[pl.ds(q * SUB + TILE * k, TILE), :] for k in range(STEPS)] for q in range(subs)]
    for m in range(MODES):
        real = [tiles[q][STEPS - 1] for q in range(subs)]
        imag = [None] * subs
        for k in range(STEPS - 1):
            by = [p8_ref[STEPS - 1 - k, c, m : m + 1, :] for c in range(2)]
            for q in range(subs):
                real[q] = real[q] + by[0] * tiles[q][k]
                term = by[1] * tiles[q][k]
                imag[q] = term if k == 0 else imag[q] + term
        for q in range(subs):
            turned = cmul((real[q], imag[q]), (r7_ref[m, 0], r7_ref[m, 1]))
            for c in range(2):
                u_ref[q, c, m : m + 1, :] = jnp.sum(turned[c], axis=0, keepdims=True)
    state = (jnp.zeros((MODES, LANES), F32),) * 2
    step = (p64_ref[1, 0], p64_ref[1, 1])
    for q in range(subs):
        for c in range(2):
            carry_ref[q, c] = state[c]
        state = cmul(state, step)
        state = (state[0] + u_ref[q, 0], state[1] + u_ref[q, 1])
    for c in range(2):
        wire_ref[MODES * c : MODES * (c + 1)] = state[c]
    send_ref[...] = wire_ref[...].astype(send_ref.dtype)


def edges(filt_ref, first, rim):
    def stream(g, own, old):
        taps = [filt_ref[3 * g + j : 3 * g + j + 1] for j in range(3)]
        return (
            taps[0] * own[0] + taps[1] * old[1] + taps[2] * old[0],
            taps[0] * own[1] + taps[1] * own[0] + taps[2] * old[1],
        )

    keys = stream(1, first[:2], rim[:2])
    values = stream(2, first[2:], rim[2:4])
    return keys[0] * values[0], keys[1] * values[1]


def lines(ref, at, count):
    return [ref[at + i : at + i + 1] for i in range(count)]


def impulses(plane_ref, at, pair):
    return [plane_ref[at, c] * pair[0] + plane_ref[at + 1, c] * pair[1] for c in range(2)]


def gathered(wide_ref, plane_ref, at, filt_ref, tables, alone):
    zero = jnp.zeros((MODES, LANES), F32)
    sums = [[zero, zero] for _ in tables]
    for i in range(wide_ref.shape[0]):
        value = [wide_ref[i, 0:MODES], wide_ref[i, MODES:HEAD]]
        if i or alone:
            rim = lines(wide_ref.at[i - 1], TAIL, 4) if i else [0.0] * 4
            extra = impulses(plane_ref, at, edges(filt_ref, lines(wide_ref.at[i], HEAD, 4), rim))
            value = [value[0] + extra[0], value[1] + extra[1]]
        for total, table_ref in zip(sums, tables):
            term = cmul(value, (table_ref[i, 0], table_ref[i, 1]))
            total[0], total[1] = total[0] + term[0], total[1] + term[1]
    return sums


def gate_kernel(a_ref, b_ref, c_ref, d_ref, scale_ref, filt_ref, _, gate_ref, ext_ref):
    gate_ref[...] = stream((a_ref, b_ref, c_ref, d_ref), 0, scale_ref, filt_ref, 0, ext_ref)


def plane_kernel(
    here_ref, next_ref, across_ref, before_ref, mine_tab_ref, all_tab_ref, plane_ref, filt_ref,
    mine_ref, rim_ref, send_ref, wide_ref, wire_ref,
):
    place = lax.rem(lax.axis_index("seq"), LOW)
    chip, core = lax.div(place, 2), lax.rem(place, 2)
    for i, ref in enumerate((here_ref, next_ref, across_ref, before_ref)):
        first = 2 * lax.rem(chip + i, LOW // 2)
        wide_ref[first + core] = ref[0].astype(F32)
        wide_ref[first + 1 - core] = ref[1].astype(F32)
    mine, total = gathered(wide_ref, plane_ref, 3, filt_ref, (mine_tab_ref, all_tab_ref), False)
    near = wide_ref[jnp.maximum(place - 1, 0), TAIL : TAIL + TILE]
    rim_ref[0] = jnp.where(place > 0, near, 0.0)
    rim_ref[1] = wide_ref[0, HEAD : HEAD + TILE]
    for c in range(2):
        mine_ref[c] = mine[c]
        wire_ref[c * MODES : (c + 1) * MODES] = total[c]
    wire_ref[HEAD:TAIL] = wide_ref[0, HEAD:TAIL]
    wire_ref[TAIL:] = wide_ref[LOW - 1, TAIL:]
    wire = wire_ref[...].astype(send_ref.dtype)
    for i in range(PLANES):
        send_ref[i] = wire


def final_kernel(
    got_ref, far_tab_ref, rim_ref, plane_ref, filt_ref, mine_ref, carry_ref, p64_ref, p8_ref, gt_ref, gate_ref, local_ref,
    head_ref, skip_ref, before_ref, out_ref, wide_ref, e_ref, y_ref, fix_ref,
):
    rows = gate_ref.shape[0]
    subs = rows // SUB
    for i in range(PLANES):
        wide_ref[i] = got_ref[i].astype(F32)
    (far,) = gathered(wide_ref, plane_ref, 5, filt_ref, (far_tab_ref,), True)
    far = cmul(far, (plane_ref[0, 0], plane_ref[0, 1]))
    block = lax.axis_index("seq")
    place, plane = lax.rem(block, LOW), lax.div(block, LOW)
    old = jnp.where(plane > 0, wide_ref[jnp.maximum(plane - 1, 0), TAIL : TAIL + TILE], 0.0)
    extra = impulses(plane_ref, 3, edges(filt_ref, lines(rim_ref.at[1], 0, 4), [old[i : i + 1] for i in range(4)]))
    near = cmul(extra, (plane_ref[1, 0], plane_ref[1, 1]))
    rim = rim_ref[0] + jnp.where(place > 0, 0.0, old)
    old = {1: (rim[0:1], rim[1:2]), 2: (rim[2:3], rim[3:4]), 0: (rim[4:5], rim[5:6])}
    late = {}
    for g in range(3):
        taps = [filt_ref[3 * g + j : 3 * g + j + 1] for j in range(3)]
        late[g] = (taps[1] * old[g][1] + taps[2] * old[g][0], taps[2] * old[g][1])
    pair = [
        (head_ref[i : i + 1] + late[1][i]) * (head_ref[2 + i : 3 + i] + late[2][i]) for i in range(2)
    ]
    own = impulses(plane_ref, 7, pair)
    enter = [mine_ref[c] + near[c] + far[c] + own[c] for c in range(2)]
    fix_ref[...] = jnp.zeros_like(fix_ref)
    for i in range(2):
        fix_ref[0, i : i + 1] = late[0][i]
        fix_ref[1, i : i + 1] = skip_ref[...] * pair[i]
    fix_ref[1, 0:1] -= before_ref[...] * pair[1]
    for q in range(subs):
        moved = cmul(enter, (p64_ref[q, 0], p64_ref[q, 1])) if q else enter
        for c in range(2):
            e_ref[q, c] = moved[c] + carry_ref[q, c]
    sums = [[None] * STEPS for _ in range(subs)]
    for m in range(MODES):
        table = (gt_ref[m, 0], gt_ref[m, 1])
        value = [cmul(table, (e_ref[q, 0, m : m + 1, :], e_ref[q, 1, m : m + 1, :])) for q in range(subs)]
        for k in range(STEPS):
            if k:
                by = [p8_ref[k, c, m : m + 1, :] for c in range(2)]
            for q in range(subs):
                term = by[0] * value[q][0] - by[1] * value[q][1] if k else value[q][0]
                sums[q][k] = term if m == 0 else sums[q][k] + term
    for q in range(subs):
        for k in range(STEPS):
            at = pl.ds(q * SUB + TILE * k, TILE)
            gate, conv = gate_ref[at, :], local_ref[at, :] + sums[q][k]
            if q == 0 and k == 0:
                gate, conv = gate + fix_ref[0], conv + fix_ref[1]
            y_ref[at, :] = gate * conv
    out_ref[...] = y_ref[...].T.astype(BF16)


def body(tokens, norm_gain, in_weight, short_filter, decay_reach, mode_freq, residues, skip_gain):
    rows, cols = tokens.shape
    fsdp = lax.axis_size("fsdp")
    state = shape(2, MODES, LANES)

    packed = 2 * rows + EXTRA
    weight = jnp.transpose(in_weight, (1, 0, 2))
    block = shape(packed, LANES, dtype=BF16)

    def exchange(own, *parts):
        sent = {
            d: lax.ppermute(parts[d - 1], "fsdp", [(i, (i + d) % fsdp) for i in range(fsdp)]) for d in (2, 1, 3)
        }
        return own, sent[1], sent[2], sent[3]

    products = call(
        project_kernel,
        (shape(packed, LANES), block, block, block, shape(rows, LANES), *[shape(rows, LANES, dtype=BF16)] * 3),
        (tokens, pltpu.with_memory_space_constraint(norm_gain[None], pltpu.HBM), weight),
        [
            pltpu.VMEM((rows, cols), BF16),
            pltpu.VMEM((1, cols), F32),
            pltpu.VMEM((3, cols, 4 * LANES), BF16),
            pltpu.VMEM((rows, cols), BF16),
            pltpu.VMEM((rows, LANES), F32),
            pltpu.VMEM((EXTRA, LANES), F32),
            pltpu.VMEM((rows, 4 * LANES), F32),
            pltpu.SemaphoreType.DMA((9,)),
            pltpu.SemaphoreType.DMA((3,)),
        ],
        limit=52 << 20,
        flops=2 * rows * cols * 12 * LANES,
        places=[HBM] * 3,
    )
    pair = exchange(*products[:4])
    gates = exchange(*products[4:])
    p8, r7, gt, p64, mine_tab, all_tab, far_tab, plane_tab, taps, before = call(
        table_kernel,
        (
            shape(STEPS, 2, MODES, LANES),
            shape(MODES, 2, TILE, LANES),
            shape(MODES, 2, TILE, LANES),
            shape(4, 2, MODES, LANES),
            shape(LOW, 2, MODES, LANES),
            shape(LOW, 2, MODES, LANES),
            shape(PLANES, 2, MODES, LANES),
            shape(9, 2, MODES, LANES),
            shape(SUB, LANES),
            shape(1, LANES),
        ),
        (decay_reach.T, mode_freq.T, residues.T),
        [pltpu.VMEM((2 * LOW, 2, MODES, LANES), F32)],
        flops=1 << 27,
    )
    filt = jnp.transpose(short_filter, (1, 2, 0)).reshape(9, LANES)
    skip = skip_gain[None]
    wire = shape(LOW, WIRE, LANES, dtype=BF16)
    scale, signal, carry, send, head = call(
        signal_kernel,
        (
            shape(rows, LANES), shape(rows, LANES), shape(4, 2, MODES, LANES),
            shape(WIRE, LANES, dtype=BF16), shape(TILE, LANES),
        ),
        (*pair, filt, p8, r7, p64),
        [
            pltpu.VMEM((2, TILE + rows, LANES), F32),
            pltpu.VMEM((4, 2, MODES, LANES), F32),
            pltpu.VMEM((WIRE, LANES), F32),
        ],
        flops=1 << 27,
    )
    blocks = range(LOW * PLANES)
    here = jnp.stack([send, lax.ppermute(send, "seq", [(i, i ^ 1) for i in blocks])])

    def ahead(d):
        return lax.ppermute(here, "seq", [(i, i // LOW * LOW + (i - 2 * d) % LOW) for i in blocks])

    near = [ahead(d) for d in (2, 1, 3)]
    mine, rim, send = call(
        plane_kernel,
        (state, shape(2, TILE, LANES), wire),
        (here, near[1], near[0], near[2], mine_tab, all_tab, plane_tab, filt),
        [pltpu.VMEM((LOW, WIRE, LANES), F32), pltpu.VMEM((WIRE, LANES), F32)],
        flops=1 << 24,
    )
    local_part = call(
        local_kernel,
        shape(rows, LANES),
        (signal, skip, taps, rim),
        [pltpu.VMEM((TILE + SUB, LANES), F32)],
        flops=1 << 27,
    )
    gate = call(
        gate_kernel,
        shape(rows, LANES),
        (*gates, scale, filt, local_part),
        [pltpu.VMEM((TILE + rows, LANES), F32)],
        flops=1 << 24,
    )
    line = [[LOW * j + g for j in range(PLANES)] for g in range(LOW)]
    got = lax.all_to_all(send, "seq", 0, 0, axis_index_groups=line)
    return call(
        final_kernel,
        shape(LANES, rows, dtype=BF16),
        (got, far_tab, rim, plane_tab, filt, mine, carry, p64, p8, gt, gate, local_part, head, skip, before),
        [
            pltpu.VMEM((PLANES, WIRE, LANES), F32),
            pltpu.VMEM((4, 2, MODES, LANES), F32),
            pltpu.VMEM((rows, LANES), F32),
            pltpu.VMEM((2, TILE, LANES), F32),
        ],
        flops=1 << 27,
    )


def solution(mesh):
    placed = (
        P("seq", "fsdp"),
        P("fsdp"),
        P("fsdp", None, None),
        P("fsdp", None, None),
        P("fsdp", None),
        P("fsdp", None),
        P("fsdp", None),
        P("fsdp"),
    )
    return jax.shard_map(
        body, mesh=mesh, in_specs=placed, out_specs=P("fsdp", "seq"), check_vma=False
    )
```
